32 devices in a mesh: grp: 2 (over y), frame: 4 (over x, core), band: 4 (over z).
Axes of the slice: x: 2, y: 2, z: 4, core: 2. Of those that a mesh axis runs over, the one named last changes fastest.
Arguments:
- features: bfloat16 [16, 64, 128, 256], P(('grp', 'frame'), 'band'), parts along dimension 0, may hold values from -6 to 6
- space_kernel: bfloat16 [3, 3, 256, 256], replicated, may hold values from -0.125 to 0.125
- space_gain: float32 [256], replicated, may hold values from 0.5 to 2
- space_bias: float32 [256], replicated, may hold values from -3 to 3
- time_kernel: bfloat16 [3, 256, 256], replicated, may hold values from -0.21875 to 0.21875
- time_gain: float32 [256], replicated, may hold values from 0.5 to 2
- time_bias: float32 [256], replicated, may hold values from -3 to 3
Outputs:
- decoded: bfloat16 [16, 64, 128, 256], P(('grp', 'frame'), 'band'), parts along dimension 0
The draws below stay inside these ranges and needn't reach their ends.
There are 2 independent parts, one for each index of `grp`. The reference program is written for one: setup_inputs(seed, part) draws one part's arguments, and reference() takes and returns one part's arrays. A program takes and returns all parts, laid end to end along the dimension named above; an argument that names none is the same for every part. Nothing has to cross between parts.
All inputs are finite; a program needn't handle non-finite values.
Results may differ from the reference program's by a relative error of at most 0.0056.
Values may be sent and summed in bfloat16 or wider, within the bound.
No kernel may reach another device: no remote copies, remote signals or barrier semaphores. Data moves between devices by JAX's collectives and lax.ppermute only.
A program may use at most 64 MiB of HBM per device.

```python
import math
import jax
import jax.numpy as jnp
from jax import lax

C = 256
W = 128
F = 8
H = 64


def block_scale(rng, shape, split, low, high):
    factor_of, own = 1.0, jax.random.fold_in(rng, 6)
    for dim, shards_of in split:
        heights = jnp.exp(jax.random.uniform(jax.random.fold_in(own, dim), (shards_of,), jnp.float32, low / len(split), high / len(split)))
        factor_of = factor_of * jnp.repeat(heights, shape[dim] // shards_of).reshape([-1 if axis == dim else 1 for axis in range(len(shape))])
    return factor_of


def bell_draw(key, shape, scale, limit, shards=(), kind=jnp.bfloat16):
    entries = jax.random.normal(key, shape, jnp.float32) * scale
    if len(shards) > 0:
        entries = block_scale(key, shape, shards, -0.22, 0.18) * entries
    return jnp.clip(entries, min=-limit, max=limit).astype(kind)


def setup_inputs(seed: int = 0, part: int = 0) -> dict:
    keys = jax.random.split(jax.random.key(seed), 8)
    own_keys = jax.random.split(jax.random.fold_in(keys[7], part), 8)
    features = bell_draw(own_keys[0], (F, H, W, C), 1.0, 6.0, ((0, 4), (1, 4)))
    space_kernel = bell_draw(keys[1], (3, 3, C, C), (9 * C) ** -0.5, 0.125)
    space_gain = jnp.clip(jnp.exp(jax.random.uniform(keys[2], (C,), jnp.float32, math.log(0.5), math.log(2.0))), 0.5, 2.0)
    space_bias = bell_draw(keys[3], (C,), 0.5, 3.0, (), jnp.float32)
    time_kernel = bell_draw(keys[4], (3, C, C), (3 * C) ** -0.5, 0.21875)
    time_gain = jnp.clip(jnp.exp(jax.random.uniform(keys[5], (C,), jnp.float32, math.log(0.5), math.log(2.0))), 0.5, 2.0)
    time_bias = bell_draw(keys[6], (C,), 0.5, 3.0, (), jnp.float32)
    return {"features": features, "space_kernel": space_kernel, "space_gain": space_gain, "space_bias": space_bias, "time_kernel": time_kernel, "time_gain": time_gain, "time_bias": time_bias}


def rms_silu(values, gain_vector):
    widened = values.astype(jnp.float32)
    scaled = widened * lax.rsqrt(lax.optimization_barrier(jnp.mean(widened * widened, axis=-1, keepdims=True)) + 1e-06) * gain_vector
    return jax.nn.silu(scaled).astype(jnp.bfloat16)

def spatial_frame(normed_frame, kernel):
    rows_count, cols_count, channels = normed_frame.shape
    padded = jnp.pad(normed_frame, ((1, 1), (1, 1), (0, 0)))
    summed = jnp.zeros((rows_count * cols_count, kernel.shape[3]), jnp.float32)
    for tap_row in range(3):
        for tap_col in range(3):
            window = padded[tap_row:tap_row + rows_count, tap_col:tap_col + cols_count].reshape(-1, channels)
            summed = summed + jnp.dot(window, kernel[tap_row, tap_col], preferred_element_type=jnp.float32)
    return summed.reshape(rows_count, cols_count, -1)

def reference(features, space_kernel, space_gain, space_bias, time_kernel, time_gain, time_bias):
    normed = rms_silu(features, space_gain)
    spatial = lax.map(lambda frame_data: spatial_frame(frame_data, space_kernel), normed)
    hidden = (features.astype(jnp.float32) + spatial + space_bias).astype(jnp.bfloat16)
    hidden = lax.optimization_barrier(hidden)
    normed_time = rms_silu(hidden, time_gain)
    frame_count = normed_time.shape[0]
    channels = normed_time.shape[-1]
    extended = jnp.pad(normed_time, ((2, 0), (0, 0), (0, 0), (0, 0)))
    summed = jnp.zeros((normed_time.size // channels, channels), jnp.float32)
    for time_lag in range(3):
        window = extended[2 - time_lag:2 - time_lag + frame_count].reshape(-1, channels)
        summed = summed + jnp.dot(window, time_kernel[time_lag], preferred_element_type=jnp.float32)
    temporal = summed.reshape(normed_time.shape).astype(jnp.bfloat16)
    temporal = lax.optimization_barrier(temporal)
    decoded = hidden.astype(jnp.float32) + temporal.astype(jnp.float32) + time_bias
    return decoded.astype(jnp.bfloat16)
```

```python
import functools

import jax
import jax.numpy as jnp
from jax import lax
from jax.experimental import pallas as pl
from jax.experimental.pallas import tpu as pltpu
from jax.sharding import PartitionSpec as P

F32 = jnp.float32
BF16 = jnp.bfloat16


def half_silu(values, half_gain):
    mean_square = jnp.mean(values * values, axis=-1, keepdims=True)
    u = values * lax.rsqrt(mean_square + 1e-06) * half_gain
    return u + u * jnp.tanh(u)


def norm_into(shifted, place, row, half_gain):
    normed = half_silu(row.astype(F32), half_gain)
    cols = normed.shape[0]
    column = lax.broadcasted_iota(jnp.int32, normed.shape, 0)
    before = jnp.where(column == 0, 0.0, pltpu.roll(normed, 1, 0))
    after = jnp.where(column == cols - 1, 0.0, pltpu.roll(normed, cols - 1, 0))
    shifted[0, place] = before.astype(BF16)
    shifted[1, place] = normed.astype(BF16)
    shifted[2, place] = after.astype(BF16)


def conv_rows(shifted, kernel, first, count):
    _, _, cols, channels = shifted.shape
    total = None
    for i in range(3):
        for j in range(3):
            window = shifted[j, first + i : first + i + count].reshape(count * cols, channels)
            product = jnp.dot(window, kernel[i, j], preferred_element_type=F32)
            total = product if total is None else total + product
    return total


def spatial_rows(get_row, rows, step, shifted, kernel, space_half, space_bias, time_half, emit):
    channels = shifted.shape[-1]
    ready = 0
    for first in range(0, rows, step):
        while ready < first + step + 2:
            norm_into(shifted, ready, get_row(ready - 1), space_half)
            ready += 1
        total = conv_rows(shifted, kernel, first, step)
        own = jnp.concatenate([get_row(r) for r in range(first, first + step)], axis=0)
        hidden = (own.astype(F32) + total + space_bias).astype(BF16)
        emit(first, hidden, half_silu(hidden.astype(F32), time_half))


def own_kernel(frame, step, feats, above, below, kernel, space_half, space_bias, time_half,
               hidden_ref, *rest):
    *normed_refs, shifted = rest
    rows = feats.shape[1]

    def get_row(r):
        if r < 0:
            return above[frame]
        if r >= rows:
            return below[frame]
        return feats[0, r]

    starts = []
    for ref in normed_refs:
        starts.append(sum(other.shape[0] for other in normed_refs[: len(starts)]))

    def emit(first, hidden, normed):
        cols, channels = feats.shape[2:]
        hidden_ref[first : first + step] = hidden.reshape(step, cols, channels)
        which = max(n for n, s in enumerate(starts) if s <= first)
        at = first - starts[which]
        normed_refs[which][at : at + step] = normed.astype(BF16).reshape(step, cols, channels)

    spatial_rows(get_row, rows, step, shifted, kernel[...], space_half[...], space_bias[...],
                 time_half[...], emit)


def joint_kernel(step, valid, edge, inner, above, below, kernel, space_half, space_bias, time_half,
                 time_kernel, time_bias, hidden_b, normed_b, *rest):
    *normed_a, out_ref, partial, shifted = rest
    rows, cols, channels = hidden_b.shape
    starts = []
    for ref in normed_a:
        starts.append(sum(other.shape[0] for other in normed_a[: len(starts)]))
    keep = valid[0]

    def get_row(r):
        if r < 0:
            return above[2]
        if r >= rows:
            return below[2]
        if r == 0:
            return edge[0]
        if r == rows - 1:
            return edge[1]
        return inner[r - 1]

    def flat(ref, first):
        return ref[first : first + step].reshape(step * cols, channels)

    def emit(first, hidden, normed):
        prior = jnp.where(keep > 0, normed, 0.0).astype(BF16)
        which = max(n for n, s in enumerate(starts) if s <= first)
        before = flat(normed_a[which], first - starts[which])
        total = jnp.dot(flat(normed_b, first), time_kernel[0], preferred_element_type=F32)
        total += jnp.dot(before, time_kernel[1], preferred_element_type=F32)
        total += jnp.dot(prior, time_kernel[2], preferred_element_type=F32)
        temporal = total.astype(BF16).astype(F32)
        decoded = flat(hidden_b, first).astype(F32) + temporal + time_bias[...]
        out_ref[0, first : first + step] = decoded.astype(BF16).reshape(step, cols, channels)
        other = jnp.dot(before, time_kernel[0], preferred_element_type=F32)
        other += jnp.dot(prior, time_kernel[1], preferred_element_type=F32)
        partial[first : first + step] = other.reshape(step, cols, channels)

    spatial_rows(get_row, rows, step, shifted, kernel[...], space_half[...], space_bias[...],
                 time_half[...], emit)


def last_kernel(arrived, partial, hidden, time_kernel, time_bias, _, out_ref):
    count, cols, channels = arrived.shape
    total = partial[...].reshape(count * cols, channels)
    total += jnp.dot(arrived[...].reshape(count * cols, channels), time_kernel[0],
                     preferred_element_type=F32)
    temporal = total.astype(BF16).astype(F32)
    decoded = hidden[...].reshape(count * cols, channels).astype(F32) + temporal + time_bias[...]
    out_ref[0] = decoded.astype(BF16).reshape(count, cols, channels)


def whole(shape):
    return pl.BlockSpec(shape, lambda *_: (0,) * len(shape))


def chunks_of(rows):
    head = rows - rows // 4
    return (head, rows - head)


def body(features, space_kernel, space_gain, space_bias, time_kernel, time_gain, time_bias):
    frames, rows, cols, channels = features.shape
    row_shape = (cols, channels)
    step = 2
    sizes = chunks_of(rows)
    pixels = rows * cols
    count_f, count_b = lax.axis_size("frame"), lax.axis_size("band")
    onward = [(i, i + 1) for i in range(count_f - 1)]
    up = [(i, i + 1) for i in range(count_b - 1)]
    down = [(j, i) for i, j in up]
    params = pltpu.CompilerParams(vmem_limit_bytes=32 * 1024 * 1024)
    flops_conv = 2 * 9 * pixels * channels * channels

    space_half = (0.5 * space_gain).reshape(1, channels)
    time_half = (0.5 * time_gain).reshape(1, channels)
    space_bias = space_bias.reshape(1, channels)
    time_bias = time_bias.reshape(1, channels)
    valid = (lax.axis_index("frame") > 0).astype(jnp.int32).reshape(1)

    last = features[1]
    edge = lax.ppermute(jnp.stack([last[0], last[rows - 1]]), "frame", onward)
    inner = lax.ppermute(last[1 : rows - 1], "frame", onward)
    above = lax.ppermute(
        jnp.concatenate([features[:, rows - 1], edge[1:]], axis=0), "band", up
    )
    below = lax.ppermute(jnp.concatenate([features[:, 0], edge[:1]], axis=0), "band", down)

    def own(frame, parts):
        return pl.pallas_call(
            functools.partial(own_kernel, frame, step),
            grid=(1,),
            in_specs=[
                pl.BlockSpec((1, rows) + row_shape, lambda *_: (frame, 0, 0, 0)),
                whole(above.shape), whole(below.shape), whole(space_kernel.shape),
                whole(space_half.shape), whole(space_bias.shape), whole(time_half.shape),
            ],
            out_specs=[whole((rows,) + row_shape)] + [whole((n,) + row_shape) for n in parts],
            out_shape=[jax.ShapeDtypeStruct((n,) + row_shape, BF16) for n in (rows,) + parts],
            scratch_shapes=[pltpu.VMEM((3, rows + 2) + row_shape, BF16)],
            compiler_params=params,
            cost_estimate=pl.CostEstimate(
                flops=flops_conv, bytes_accessed=5 * pixels * channels * 2, transcendentals=2 * pixels * channels
            ),
            name=f"own_frame_{frame}",
        )(features, above, below, space_kernel, space_half, space_bias, time_half)

    hidden_a, *normed_a = own(0, sizes)
    arrived = [lax.ppermute(part, "frame", onward) for part in normed_a]
    hidden_b, normed_b = own(1, (rows,))

    inputs = [valid, edge, inner, above, below, space_kernel, space_half, space_bias, time_half,
              time_kernel, time_bias, hidden_b, normed_b, *normed_a]
    decoded, partial = pl.pallas_call(
        functools.partial(joint_kernel, step),
        grid=(1,),
        in_specs=[pl.BlockSpec(memory_space=pltpu.SMEM)] + [whole(x.shape) for x in inputs[1:]],
        out_specs=[
            pl.BlockSpec((1, rows) + row_shape, lambda *_: (1, 0, 0, 0)),
            whole((rows,) + row_shape),
        ],
        out_shape=[
            jax.ShapeDtypeStruct(features.shape, BF16),
            jax.ShapeDtypeStruct((rows,) + row_shape, F32),
        ],
        scratch_shapes=[pltpu.VMEM((3, rows + 2) + row_shape, BF16)],
        compiler_params=params,
        cost_estimate=pl.CostEstimate(
            flops=flops_conv * 14 // 9, bytes_accessed=10 * pixels * channels * 2,
            transcendentals=2 * pixels * channels,
        ),
        name="joint",
    )(*inputs)

    first = 0
    for part in arrived:
        count = part.shape[0]
        block = next(b for b in range(min(count, 4), 0, -1) if count % b == 0 and first % b == 0)
        base = first // block
        row_block = pl.BlockSpec((block,) + row_shape, lambda i, base=base: (base + i, 0, 0))
        decoded = pl.pallas_call(
            last_kernel,
            grid=(count // block,),
            in_specs=[
                pl.BlockSpec((block,) + row_shape, lambda i: (i, 0, 0)),
                row_block, row_block,
                pl.BlockSpec((1,) + time_kernel.shape[1:], lambda i: (2, 0, 0)),
                whole(time_bias.shape),
                pl.BlockSpec(memory_space=pl.ANY),
            ],
            out_specs=pl.BlockSpec((1, block) + row_shape, lambda i, base=base: (0, base + i, 0, 0)),
            out_shape=jax.ShapeDtypeStruct(features.shape, BF16),
            input_output_aliases={5: 0},
            compiler_params=params,
            cost_estimate=pl.CostEstimate(
                flops=2 * count * cols * channels * channels,
                bytes_accessed=10 * count * cols * channels, transcendentals=0,
            ),
            name="finish",
        )(part, partial, hidden_a, time_kernel, time_bias, decoded)
        first += count
    return decoded


def solution(mesh):
    return jax.shard_map(
        body,
        mesh=mesh,
        in_specs=(P(("grp", "frame"), "band", None, None), P(), P(), P(), P(), P(), P()),
        out_specs=P(("grp", "frame"), "band", None, None),
        check_vma=False,
    )
```

```python
import functools

import jax
import jax.numpy as jnp
from jax import lax
from jax.experimental import pallas as pl
from jax.experimental.pallas import tpu as pltpu
from jax.sharding import PartitionSpec as P

F32 = jnp.float32
BF16 = jnp.bfloat16
VMEM = pl.BlockSpec(memory_space=pltpu.VMEM)
SMEM = pl.BlockSpec(memory_space=pltpu.SMEM)
ANY = pl.BlockSpec(memory_space=pl.ANY)
HBM = pl.BlockSpec(memory_space=pltpu.HBM)
STEP = 2


def blocks(first, last):
    return [(r, min(STEP, last - r)) for r in range(first, last, STEP)]


def half_silu(values, half_gain):
    mean_square = jnp.mean(values * values, axis=-1, keepdims=True)
    u = values * lax.rsqrt(mean_square + 1e-06) * half_gain
    return u + u * jnp.tanh(u)


def norm_into(shifted, place, row, half_gain):
    normed = half_silu(row.astype(F32), half_gain)
    cols = normed.shape[0]
    column = lax.broadcasted_iota(jnp.int32, normed.shape, 0)
    before = jnp.where(column == 0, 0.0, pltpu.roll(normed, 1, 0))
    after = jnp.where(column == cols - 1, 0.0, pltpu.roll(normed, cols - 1, 0))
    shifted[0, place] = before.astype(BF16)
    shifted[1, place] = normed.astype(BF16)
    shifted[2, place] = after.astype(BF16)


def conv_rows(shifted, kernel, place, count):
    cols, channels = shifted.shape[2:]
    total = None
    for i in range(3):
        for j in range(3):
            window = shifted[j, place + i : place + i + count].reshape(count * cols, channels)
            product = jnp.dot(window, kernel[i, j], preferred_element_type=F32)
            total = product if total is None else total + product
    return total


def spatial_jobs(get_row, row_blocks, offset, shifted, sums, slot0, kernel, weights, emit, after=None):
    space_half, space_bias, time_half = weights
    ready = set()
    jobs = []

    def norm_stage(first, count):
        for r in range(first - 1, first + count + 1):
            if r not in ready:
                ready.add(r)
                norm_into(shifted, r + offset, get_row(r), space_half[...])

    def conv_stage(slot, first, count):
        total = conv_rows(shifted, kernel, first - 1 + offset, count)
        sums[slot, : total.shape[0]] = total

    def emit_stage(slot, first, count):
        own = jnp.concatenate([get_row(r) for r in range(first, first + count)], axis=0)
        hidden = own.astype(F32) + sums[slot, : own.shape[0]] + space_bias[...]
        emit(first, count, hidden, half_silu(hidden, time_half[...]))

    for n, (first, count) in enumerate(row_blocks):
        slot = (slot0 + n) % sums.shape[0]
        jobs.append([
            functools.partial(norm_stage, first, count),
            functools.partial(conv_stage, slot, first, count),
            functools.partial(emit_stage, slot, first, count),
            functools.partial(after, first, count) if after else None,
        ])
    return jobs


def run(jobs):
    for n in range(len(jobs) + 3):
        for stage in range(4):
            if 0 <= n - stage < len(jobs) and jobs[n - stage][stage] is not None:
                jobs[n - stage][stage]()


def split_kernel(feats, edge, inner, tops, bottoms, sems):
    rows = feats.shape[1]
    pairs = [
        (feats.at[1, pl.ds(0, 1)], edge.at[pl.ds(0, 1)]),
        (feats.at[1, pl.ds(rows - 1, 1)], edge.at[pl.ds(1, 1)]),
        (feats.at[pl.ds(0, 2), 0], tops),
        (feats.at[pl.ds(0, 2), rows - 1], bottoms),
        (feats.at[1, pl.ds(1, rows - 2)], inner),
    ]
    copies = [pltpu.make_async_copy(a, b, sems.at[n]) for n, (a, b) in enumerate(pairs)]
    for copy in copies:
        copy.start()
    for copy in copies:
        copy.wait()


def interior_kernel(feats, kernel, time_kernel, space_half, space_bias, time_half,
                    hidden_ref, normed_ref, raw, kernel_out, time_out, shifted, sums, sems):
    rows, cols, channels = raw.shape
    half = rows // 2
    pairs = [
        (feats.at[0, pl.ds(0, half)], raw.at[pl.ds(0, half)]),
        (kernel, kernel_out),
        (feats.at[0, pl.ds(half, rows - half)], raw.at[pl.ds(half, rows - half)]),
        (time_kernel, time_out),
    ]
    copies = [pltpu.make_async_copy(a, b, sems.at[n]) for n, (a, b) in enumerate(pairs)]
    for copy in copies:
        copy.start()

    def emit(first, count, hidden, normed):
        shape = (count, cols, channels)
        hidden_ref[first - 1 : first - 1 + count] = hidden.astype(BF16).reshape(shape)
        normed_ref[first - 1 : first - 1 + count] = normed.astype(BF16).reshape(shape)

    jobs = spatial_jobs(lambda r: raw[r], blocks(1, rows - 1), 0, shifted, sums, 0, kernel_out,
                        (space_half, space_bias, time_half), emit)
    copies[0].wait()
    jobs[0][0]()
    jobs[0][0] = None
    for copy in copies[1:]:
        copy.wait()
    run(jobs)


def main_kernel(valid, raw_a, own_edge, own_inner, edge, inner, above, below, kernel, space_half, space_bias, time_half,
                time_kernel, time_bias, hidden_a, normed_a,
                out_ref, base, edge_normed,
                shift_a, shift_b, shift_p, sums, hidden_b, normed_b, normed_p, hidden_e, decoded, sems):
    rows, cols, channels = raw_a.shape
    keep = valid[0]
    weights = (space_half, space_bias, time_half)

    def a_row(r):
        return above[0] if r < 0 else below[0] if r >= rows else raw_a[r]

    def framed(upper, edges, inners, lower):
        def get_row(r):
            if r < 0 or r >= rows:
                return (upper if r < 0 else lower)[...]
            return edges[0] if r == 0 else edges[1] if r == rows - 1 else inners[r - 1]
        return get_row

    def emit_a(first, count, hidden, normed):
        which = 0 if first == 0 else 1
        hidden_e[which] = hidden
        edge_normed[which] = normed.astype(BF16)

    def emit_b(first, count, hidden, normed):
        hidden_b[first : first + count] = hidden.reshape(count, cols, channels)
        normed_b[first : first + count] = normed.astype(BF16).reshape(count, cols, channels)

    def emit_p(first, count, hidden, normed):
        normed_p[first : first + count] = (normed * keep).astype(BF16).reshape(count, cols, channels)

    def rows_of(first, count, of_edge, of_inner):
        parts = []
        for r in range(first, first + count):
            parts.append(of_edge[0] if r == 0 else of_edge[1] if r == rows - 1 else of_inner[r - 1])
        return jnp.concatenate(parts, axis=0)

    def out_rows(first, count):
        size = count * cols
        before = rows_of(first, count, edge_normed, normed_a)
        mine = normed_b[first : first + count].reshape(size, channels)
        prior = normed_p[first : first + count].reshape(size, channels)
        total = hidden_b[first : first + count].reshape(size, channels) + time_bias[...]
        total += (
            jnp.dot(mine, time_kernel[0], preferred_element_type=F32)
            + jnp.dot(before, time_kernel[1], preferred_element_type=F32)
            + jnp.dot(prior, time_kernel[2], preferred_element_type=F32)
        )
        decoded[first : first + count] = total.astype(BF16).reshape(count, cols, channels)

    def base_rows(first, count):
        before = rows_of(first, count, edge_normed, normed_a)
        prior = normed_p[first : first + count].reshape(count * cols, channels)
        other = rows_of(first, count, hidden_e, hidden_a).astype(F32) + time_bias[...]
        other += (
            jnp.dot(before, time_kernel[0], preferred_element_type=F32)
            + jnp.dot(prior, time_kernel[1], preferred_element_type=F32)
        )
        base[first : first + count] = other.reshape(count, cols, channels)

    b_row = framed(above.at[1], own_edge, own_inner, below.at[1])
    p_row = framed(above.at[2], edge, inner, below.at[2])
    top = spatial_jobs(a_row, [(0, 1)], 1, shift_a.at[0], sums, 0, kernel, weights, emit_a)
    bottom = spatial_jobs(a_row, [(rows - 1, 1)], 2 - rows, shift_a.at[1], sums, 1, kernel,
                          weights, emit_a)
    mine = spatial_jobs(b_row, blocks(0, rows), 1, shift_b, sums, 2, kernel, weights, emit_b)
    prior = spatial_jobs(p_row, blocks(0, rows), 1, shift_p, sums, 2 + len(mine), kernel,
                         weights, emit_p)
    run(top + bottom + mine + prior)
    copies = []
    for n, (first, count) in enumerate(blocks(0, rows)):
        out_rows(first, count)
        copies.append(pltpu.make_async_copy(
            decoded.at[pl.ds(first, count)], out_ref.at[1, pl.ds(first, count)], sems.at[n]))
        copies[-1].start()
    for first, count in blocks(0, rows):
        base_rows(first, count)
    for copy in copies:
        copy.wait()


def finish_kernel(places, arrived, base, time_kernel, _, out_ref, decoded, sems):
    cols, channels = arrived.shape[1:]
    copies = []
    for n, (at, row, count) in enumerate(places):
        total = base[row : row + count].reshape(count * cols, channels)
        total += jnp.dot(arrived[at : at + count].reshape(count * cols, channels), time_kernel[2],
                         preferred_element_type=F32)
        decoded[at : at + count] = total.astype(BF16).reshape(count, cols, channels)
        copies.append(pltpu.make_async_copy(
            decoded.at[pl.ds(at, count)], out_ref.at[0, pl.ds(row, count)], sems.at[n]))
        copies[-1].start()
    for copy in copies:
        copy.wait()


def cost(pixels, taps, channels, arrays):
    return pl.CostEstimate(
        flops=2 * pixels * taps * channels * channels,
        bytes_accessed=2 * arrays * pixels * channels,
        transcendentals=2 * pixels * channels,
    )


def body(features, space_kernel, space_gain, space_bias, time_kernel, time_gain, time_bias):
    frames, rows, cols, channels = features.shape
    row = (cols, channels)
    count_f, count_b = lax.axis_size("frame"), lax.axis_size("band")
    onward = [(i, i + 1) for i in range(count_f - 1)]
    up = [(i, i + 1) for i in range(count_b - 1)]
    down = [(j, i) for i, j in up]

    def params(mebibytes):
        return pltpu.CompilerParams(vmem_limit_bytes=mebibytes * 1024 * 1024)

    def shape(*lead, dtype=BF16):
        return jax.ShapeDtypeStruct(tuple(lead) + row, dtype)

    def room(*lead, dtype=BF16):
        return pltpu.VMEM(tuple(lead) + row, dtype)

    space_half = (0.5 * space_gain).reshape(1, channels)
    time_half = (0.5 * time_gain).reshape(1, channels)
    space_bias = space_bias.reshape(1, channels)
    time_bias = time_bias.reshape(1, channels)
    valid = (lax.axis_index("frame") > 0).astype(F32).reshape(1)
    sums = pltpu.VMEM((4, STEP * cols, channels), F32)

    edge_out, inner_out, tops, bottoms = pl.pallas_call(
        split_kernel,
        in_specs=[HBM],
        out_specs=[VMEM] * 4,
        out_shape=[shape(2), shape(rows - 2), shape(2), shape(2)],
        scratch_shapes=[pltpu.SemaphoreType.DMA((5,))],
        compiler_params=params(2),
        name="split",
    )(pltpu.with_memory_space_constraint(features, pltpu.HBM))
    edge = lax.ppermute(edge_out, "frame", onward)
    inner = lax.ppermute(inner_out, "frame", onward)
    up_rows = jnp.concatenate([bottoms, edge[1:]], axis=0)
    down_rows = jnp.concatenate([tops, edge[:1]], axis=0)

    up_rows, down_rows, features = lax.optimization_barrier((up_rows, down_rows, features))
    above = lax.ppermute(up_rows, "band", up)
    below = lax.ppermute(down_rows, "band", down)
    hidden_a, normed_a, raw_a, space_kernel, time_kernel = pl.pallas_call(
        interior_kernel,
        in_specs=[HBM] * 3 + [VMEM] * 3,
        out_specs=[VMEM] * 5,
        out_shape=[shape(rows - 2), shape(rows - 2), shape(rows),
                   jax.ShapeDtypeStruct(space_kernel.shape, BF16),
                   jax.ShapeDtypeStruct(time_kernel.shape, BF16)],
        scratch_shapes=[room(3, rows), sums, pltpu.SemaphoreType.DMA((4,))],
        compiler_params=params(6),
        cost_estimate=cost(rows * cols, 9 * 4, channels, 3),
        name="interior",
    )(*(pltpu.with_memory_space_constraint(x, pltpu.HBM) for x in (features, space_kernel, time_kernel)),
      space_half, space_bias, time_half)
    arrived = lax.ppermute(normed_a, "frame", onward)

    inputs = [valid, raw_a, edge_out, inner_out, edge, inner, above, below, space_kernel, space_half, space_bias,
              time_half, time_kernel, time_bias, hidden_a, normed_a]
    decoded, base, edge_normed = pl.pallas_call(
        main_kernel,
        in_specs=[SMEM] + [VMEM] * (len(inputs) - 1),
        out_specs=[ANY, VMEM, VMEM],
        out_shape=[jax.ShapeDtypeStruct(features.shape, BF16), shape(rows, dtype=F32), shape(2)],
        scratch_shapes=[
            room(2, 3, 3), room(3, rows + 2), room(3, rows + 2), sums, room(rows, dtype=F32),
            room(rows), room(rows), room(2, dtype=F32), room(rows),
            pltpu.SemaphoreType.DMA((len(blocks(0, rows)),)),
        ],
        compiler_params=params(18),
        cost_estimate=cost(rows * cols, 23 * 8, channels, 10),
        name="main",
    )(*inputs)
    edge_arrived = lax.ppermute(edge_normed, "frame", onward)

    inner_places = [(r - 1, r, n) for r, n in blocks(1, rows - 1)]
    edge_places = [(0, 0, 1), (1, rows - 1, 1)]
    for part, places in ((arrived, inner_places), (edge_arrived, edge_places)):
        decoded = pl.pallas_call(
            functools.partial(finish_kernel, places),
            in_specs=[VMEM] * 3 + [ANY],
            out_specs=ANY,
            out_shape=jax.ShapeDtypeStruct(features.shape, BF16),
            scratch_shapes=[room(part.shape[0]), pltpu.SemaphoreType.DMA((len(places),))],
            input_output_aliases={3: 0},
            compiler_params=params(3),
            cost_estimate=cost(part.shape[0] * cols, 1, channels, 4),
            name="finish",
        )(part, base, time_kernel, decoded)
    return decoded


def solution(mesh):
    return jax.shard_map(
        body,
        mesh=mesh,
        in_specs=(P(("grp", "frame"), "band", None, None), P(), P(), P(), P(), P(), P()),
        out_specs=P(("grp", "frame"), "band", None, None),
        check_vma=False,
    )
```

```python
import functools

import jax
import jax.numpy as jnp
from jax import lax
from jax.experimental import pallas as pl
from jax.experimental.pallas import tpu as pltpu
from jax.sharding import PartitionSpec as P

F32 = jnp.float32
BF16 = jnp.bfloat16
VMEM = pl.BlockSpec(memory_space=pltpu.VMEM)
ANY = pl.BlockSpec(memory_space=pl.ANY)
HBM = pl.BlockSpec(memory_space=pltpu.HBM)
STEP = 2


def blocks(first, last):
    return [(r, min(STEP, last - r)) for r in range(first, last, STEP)]


def rms_silu(values, gain):
    mean_square = jnp.mean(values * values, axis=-1, keepdims=True)
    u = values * lax.rsqrt(mean_square + 1e-06) * (0.5 * gain)
    return u + u * jnp.tanh(u)


def norm_into(shifted, place, row, gain):
    row, scale = row if isinstance(row, tuple) else (row, None)
    normed = rms_silu(row.astype(F32), gain)
    normed = normed if scale is None else normed * scale
    cols = normed.shape[0]
    column = lax.broadcasted_iota(jnp.int32, normed.shape, 0)
    before = jnp.where(column == 0, 0.0, pltpu.roll(normed, 1, 0))
    after = jnp.where(column == cols - 1, 0.0, pltpu.roll(normed, cols - 1, 0))
    shifted[0, place] = before.astype(BF16)
    shifted[1, place] = normed.astype(BF16)
    shifted[2, place] = after.astype(BF16)


def conv_rows(shifted, kernel, place, count):
    cols, channels = shifted.shape[2:]
    total = None
    for i in range(3):
        for j in range(3):
            window = shifted[j, place + i : place + i + count].reshape(count * cols, channels)
            product = jnp.dot(window, kernel[i, j], preferred_element_type=F32)
            total = product if total is None else total + product
    return total


def spatial_jobs(get_row, row_blocks, offset, shifted, sums, slot0, kernel, weights, emit, after=None):
    space_gain, space_bias, time_gain = weights
    ready = set()
    jobs = []

    def norm_stage(first, count):
        for r in range(first - 1, first + count + 1):
            if r not in ready:
                ready.add(r)
                norm_into(shifted, r + offset, get_row(r), space_gain[...])

    def conv_stage(slot, first, count):
        total = conv_rows(shifted, kernel, first - 1 + offset, count)
        sums[slot, : total.shape[0]] = total

    def emit_stage(slot, first, count):
        own = jnp.concatenate([get_row(r) for r in range(first, first + count)], axis=0)
        hidden = own.astype(F32) + sums[slot, : own.shape[0]] + space_bias[...]
        emit(first, count, hidden, rms_silu(hidden, time_gain[...]))

    for n, (first, count) in enumerate(row_blocks):
        slot = (slot0 + n) % sums.shape[0]
        jobs.append([
            functools.partial(norm_stage, first, count),
            functools.partial(conv_stage, slot, first, count),
            functools.partial(emit_stage, slot, first, count),
            functools.partial(after, first, count) if after else None,
        ])
    return jobs


def run(jobs):
    for n in range(len(jobs) + 3):
        for stage in range(4):
            if 0 <= n - stage < len(jobs) and jobs[n - stage][stage] is not None:
                jobs[n - stage][stage]()


def split_kernel(first, feats, out, sems):
    rows = feats.shape[1]
    places = [(first, rows - first, 0)] if first else [(0, 1, 0), (rows - 1, rows, 1)]
    copies = [
        pltpu.make_async_copy(feats.at[1, pl.ds(a, b - a)], out.at[pl.ds(at, b - a)], sems.at[n])
        for n, (a, b, at) in enumerate(places)
    ]
    for copy in copies:
        copy.start()
    for copy in copies:
        copy.wait()


def goes_up(index, count):
    return index % 2 == 0 or count % 2 == 1


def halo_ring(frames, bands):
    paired = frames % 2 == 0
    pairs = []
    for f in range(frames):
        for b in range(bands):
            to = (f, b + 1) if goes_up(f, frames) else (f, b - 1)
            if not 0 <= to[1] < bands:
                if not paired:
                    continue
                to = (f ^ 1, b)
            pairs.append((f * bands + b, to[0] * bands + to[1]))
    return pairs


def up_first(count):
    index = lax.axis_index("frame")
    return lax.rem(index, 2) == 0 if count % 2 == 0 else index >= 0


def halo_kernel(count, raw_a, edges_b, edges, send_0, send_1):
    rows = raw_a.shape[0]

    def fill(up_rows, down_rows):
        for n, (first, last) in enumerate((
            (raw_a.at[0], raw_a.at[rows - 1]), (edges_b.at[0], edges_b.at[1]), (edges.at[0], edges.at[1])
        )):
            up_rows[n] = last[...]
            down_rows[n] = first[...]

    up = up_first(count)
    pl.when(up)(lambda: fill(send_0, send_1))
    pl.when(jnp.logical_not(up))(lambda: fill(send_1, send_0))


def halo_row(counts, got_0, got_1, n, is_above):
    frames, bands = counts
    band = lax.axis_index("band")
    take = up_first(frames) if is_above else jnp.logical_not(up_first(frames))
    row = jnp.where(take, got_0[n].astype(F32), got_1[n].astype(F32))
    there = band > 0 if is_above else band < bands - 1
    return row, jnp.where(there, 1.0, 0.0)


def framed(upper, edges, inners, lower):
    rows = inners.shape[0] + 2

    def get_row(r):
        if r < 0 or r >= rows:
            return upper() if r < 0 else lower()
        return edges[0] if r == 0 else edges[1] if r == rows - 1 else inners[r - 1]

    return get_row


def inner_emit(hidden_ref, normed_ref):
    def emit(first, count, hidden, normed):
        at = pl.ds(first - 1, count)
        shape = (count,) + hidden_ref.shape[1:]
        hidden_ref[at] = hidden.astype(hidden_ref.dtype).reshape(shape)
        normed_ref[at] = normed.astype(BF16).reshape(shape)
    return emit


def edge_emit(hidden_ref, normed_ref):
    def emit(first, count, hidden, normed):
        which = 0 if first == 0 else 1
        hidden_ref[which] = hidden
        normed_ref[which] = normed.astype(BF16)
    return emit


def inner_a_kernel(feats, kernel, time_kernel, space_gain, space_bias, time_gain,
                   hidden_ref, normed_ref, raw, kernel_out, time_out, shifted, sums, sems):
    rows = raw.shape[0]
    half = rows // 2
    pairs = [
        (feats.at[0, pl.ds(0, half)], raw.at[pl.ds(0, half)]),
        (kernel, kernel_out),
        (feats.at[0, pl.ds(half, rows - half)], raw.at[pl.ds(half, rows - half)]),
        (time_kernel, time_out),
    ]
    copies = [pltpu.make_async_copy(a, b, sems.at[n]) for n, (a, b) in enumerate(pairs)]
    for copy in copies:
        copy.start()
    jobs = spatial_jobs(lambda r: raw[r], blocks(1, rows - 1), 0, shifted, sums, 0, kernel_out,
                        (space_gain, space_bias, time_gain), inner_emit(hidden_ref, normed_ref))
    copies[0].wait()
    jobs[0][0]()
    jobs[0][0] = None
    for copy in copies[1:]:
        copy.wait()
    run(jobs)


def inner_b_kernel(edges, inners, kernel, space_gain, space_bias, time_gain,
                   hidden_ref, normed_ref, shifted, sums):
    rows = inners.shape[0] + 2
    run(spatial_jobs(framed(None, edges, inners, None), blocks(1, rows - 1), 0, shifted, sums, 0,
                     kernel, (space_gain, space_bias, time_gain), inner_emit(hidden_ref, normed_ref)))


def edges_kernel(counts, raw_a, edges_b, inners_b, got_0, got_1, kernel, space_gain, space_bias, time_gain,
                 hidden_a, normed_a, hidden_b, normed_b, shifted, sums):
    rows = raw_a.shape[0]
    weights = (space_gain, space_bias, time_gain)

    halo = functools.partial(halo_row, counts, got_0, got_1)

    def row_a(r):
        return halo(0, r < 0) if r < 0 or r >= rows else raw_a[r]

    row_b = framed(lambda: halo(1, True), edges_b, inners_b, lambda: halo(1, False))
    jobs = []
    for n, (get_row, emit) in enumerate((
        (row_a, edge_emit(hidden_a, normed_a)), (row_b, edge_emit(hidden_b, normed_b))
    )):
        for m, (r, offset) in enumerate(((0, 1), (rows - 1, 2 - rows))):
            jobs += spatial_jobs(get_row, [(r, 1)], offset, shifted.at[2 * n + m], sums, 2 * n + m,
                                 kernel, weights, emit)
    run(jobs)


def main_kernel(counts, edges, inners, got_0, got_1, kernel, space_gain, space_bias, time_gain,
                time_kernel, time_bias, hidden_ae, hidden_ai, normed_ae, normed_ai,
                hidden_be, hidden_bi, normed_be, normed_bi,
                out_ref, base, shifted, sums, normed_p, decoded, sems):
    rows, cols, channels = base.shape
    keep = jnp.where(lax.axis_index("frame") > 0, 1.0, 0.0)

    def emit(first, count, hidden, normed):
        normed_p[first : first + count] = (normed * keep).astype(BF16).reshape(count, cols, channels)

    def rows_of(first, count, *parts):
        get_row = framed(None, *parts, None)
        return jnp.concatenate([get_row(r) for r in range(first, first + count)], axis=0)

    def out_rows(first, count):
        prior = normed_p[first : first + count].reshape(count * cols, channels)
        total = rows_of(first, count, hidden_be, hidden_bi) + time_bias[...]
        total += (
            jnp.dot(rows_of(first, count, normed_be, normed_bi), time_kernel[0], preferred_element_type=F32)
            + jnp.dot(rows_of(first, count, normed_ae, normed_ai), time_kernel[1], preferred_element_type=F32)
            + jnp.dot(prior, time_kernel[2], preferred_element_type=F32)
        )
        decoded[first : first + count] = total.astype(BF16).reshape(count, cols, channels)

    def base_rows(first, count):
        prior = normed_p[first : first + count].reshape(count * cols, channels)
        total = rows_of(first, count, hidden_ae, hidden_ai) + time_bias[...]
        total += (
            jnp.dot(rows_of(first, count, normed_ae, normed_ai), time_kernel[0], preferred_element_type=F32)
            + jnp.dot(prior, time_kernel[1], preferred_element_type=F32)
        )
        base[first : first + count] = total.reshape(count, cols, channels)

    halo = functools.partial(halo_row, counts, got_0, got_1, 2)
    get_row = framed(lambda: halo(True), edges, inners, lambda: halo(False))
    run(spatial_jobs(get_row, blocks(0, rows), 1, shifted, sums, 0, kernel,
                     (space_gain, space_bias, time_gain), emit))
    copies = []
    for n, (first, count) in enumerate(blocks(0, rows)):
        out_rows(first, count)
        copies.append(pltpu.make_async_copy(
            decoded.at[pl.ds(first, count)], out_ref.at[1, pl.ds(first, count)], sems.at[n]))
        copies[-1].start()
    for first, count in blocks(0, rows):
        base_rows(first, count)
    for copy in copies:
        copy.wait()


def finish_kernel(places, arrived, base, time_kernel, _, out_ref, decoded, sems):
    cols, channels = base.shape[1:]
    keep = jnp.where(lax.axis_index("frame") > 0, 1.0, 0.0)
    kernel = (time_kernel[2].astype(F32) * keep).astype(BF16)
    copies = []
    for n, (at, row, count) in enumerate(places):
        total = base[row : row + count].reshape(count * cols, channels)
        total += jnp.dot(arrived[at : at + count].reshape(count * cols, channels), kernel,
                         preferred_element_type=F32)
        decoded[at : at + count] = total.astype(BF16).reshape(count, cols, channels)
        copies.append(pltpu.make_async_copy(
            decoded.at[pl.ds(at, count)], out_ref.at[0, pl.ds(row, count)], sems.at[n]))
        copies[-1].start()
    for copy in copies:
        copy.wait()


def cost(pixels, taps, channels, arrays):
    return pl.CostEstimate(
        flops=2 * pixels * taps * channels * channels,
        bytes_accessed=2 * arrays * pixels * channels,
        transcendentals=2 * pixels * channels,
    )


def body(features, space_kernel, space_gain, space_bias, time_kernel, time_gain, time_bias):
    frames, rows, cols, channels = features.shape
    row = (cols, channels)
    count_f, count_b = lax.axis_size("frame"), lax.axis_size("band")
    counts = (count_f, count_b)
    onward = [(i, (i + 1) % count_f) for i in range(count_f)]
    ring = halo_ring(count_f, count_b)

    def shape(*lead, dtype=BF16):
        return jax.ShapeDtypeStruct(tuple(lead) + row, dtype)

    def room(*lead, dtype=BF16):
        return pltpu.VMEM(tuple(lead) + row, dtype)

    space_gain = space_gain.reshape(1, channels)
    time_gain = time_gain.reshape(1, channels)
    space_bias = space_bias.reshape(1, channels)
    time_bias = time_bias.reshape(1, channels)
    sums = pltpu.VMEM((4, STEP * cols, channels), F32)

    weights = (space_gain, space_bias, time_gain)
    count = len(blocks(0, rows))

    def call(kernel, inputs, outs, scratch, mebibytes, name, **more):
        inputs = [x if isinstance(x, tuple) else (VMEM, x) for x in inputs]
        specs, arrays = zip(*inputs)
        out_specs, out_shape = zip(*((VMEM, o) if not isinstance(o, tuple) else o for o in outs))
        arrays = [x if x.ndim < 3 or s is ANY else pltpu.with_memory_space_constraint(x, s.memory_space)
                  for s, x in zip(specs, arrays)]
        out_shape = [pltpu.VMEM(o.shape, o.dtype) if s is VMEM else o for s, o in zip(out_specs, out_shape)]
        return pl.pallas_call(
            kernel, in_specs=list(specs), out_specs=list(out_specs), out_shape=out_shape,
            scratch_shapes=scratch, name=name,
            compiler_params=pltpu.CompilerParams(vmem_limit_bytes=mebibytes * 1024 * 1024), **more,
        )(*arrays)

    def split(first, feats, n):
        return call(
            functools.partial(split_kernel, first), [(HBM, feats)], [shape(n)],
            [pltpu.SemaphoreType.DMA((2,))], 1, "split",
        )[0]

    edge_out = split(0, features, 2)
    edge = lax.ppermute(edge_out, "frame", onward)
    inner_out = split(1, features, rows - 2)
    inner = lax.ppermute(inner_out, "frame", onward)

    hidden_ai, normed_ai, raw_a, space_kernel, time_kernel = call(
        inner_a_kernel,
        [(HBM, features), (HBM, space_kernel), (HBM, time_kernel), *weights],
        [shape(rows - 2, dtype=F32), shape(rows - 2), shape(rows),
         jax.ShapeDtypeStruct(space_kernel.shape, BF16), jax.ShapeDtypeStruct(time_kernel.shape, BF16)],
        [room(3, rows), sums, pltpu.SemaphoreType.DMA((4,))],
        6, "inner_a", cost_estimate=cost(rows * cols, 9, channels, 3),
    )
    arrived = lax.ppermute(normed_ai, "frame", onward)

    send_0, send_1 = call(
        functools.partial(halo_kernel, count_f), [raw_a, edge_out, edge], [shape(3), shape(3)], [], 1, "halo",
    )
    got_0 = lax.ppermute(send_0, ("frame", "band"), ring)
    got_1 = lax.ppermute(send_1, ("frame", "band"), [(t, s) for s, t in ring])
    send_0, send_1, edge_b = lax.optimization_barrier((send_0, send_1, edge_out))
    hidden_bi, normed_bi = call(
        inner_b_kernel, [edge_b, inner_out, space_kernel, *weights],
        [shape(rows - 2, dtype=F32), shape(rows - 2)], [room(3, rows), sums],
        6, "inner_b", cost_estimate=cost(rows * cols, 9 * 8, channels, 3),
    )
    hidden_ae, normed_ae, hidden_be, normed_be = call(
        functools.partial(edges_kernel, counts), [raw_a, edge_out, inner_out, got_0, got_1, space_kernel, *weights],
        [shape(2, dtype=F32), shape(2)] * 2, [room(4, 3, 3), sums],
        4, "edges", cost_estimate=cost(4 * cols, 9, channels, 3),
    )
    edge_arrived = lax.ppermute(normed_ae, "frame", onward)

    decoded, base = call(
        functools.partial(main_kernel, counts),
        [edge, inner, got_0, got_1, space_kernel, *weights, time_kernel, time_bias,
         hidden_ae, hidden_ai, normed_ae, normed_ai, hidden_be, hidden_bi, normed_be, normed_bi],
        [(ANY, jax.ShapeDtypeStruct(features.shape, BF16)), shape(rows, dtype=F32)],
        [room(3, rows + 2), sums, room(rows), room(rows), pltpu.SemaphoreType.DMA((count,))],
        9, "main", cost_estimate=cost(rows * cols, 14, channels, 10),
    )
    inner_places = [(r - 1, r, n) for r, n in blocks(1, rows - 1)]
    edge_places = [(0, 0, 1), (1, rows - 1, 1)]
    for part, places in ((arrived, inner_places), (edge_arrived, edge_places)):
        decoded = call(
            functools.partial(finish_kernel, places), [part, base, time_kernel, (ANY, decoded)],
            [(ANY, jax.ShapeDtypeStruct(features.shape, BF16))],
            [room(part.shape[0]), pltpu.SemaphoreType.DMA((len(places),))],
            3, "finish", input_output_aliases={3: 0},
            cost_estimate=cost(part.shape[0] * cols, 1, channels, 4),
        )[0]
    return decoded


def solution(mesh):
    return jax.shard_map(
        body,
        mesh=mesh,
        in_specs=(P(("grp", "frame"), "band", None, None), P(), P(), P(), P(), P(), P()),
        out_specs=P(("grp", "frame"), "band", None, None),
        check_vma=False,
    )
```

```python
import functools

import jax
import jax.numpy as jnp
from jax import lax
from jax.experimental import pallas as pl
from jax.experimental.pallas import tpu as pltpu
from jax.sharding import PartitionSpec as P

F32 = jnp.float32
BF16 = jnp.bfloat16
VMEM = pl.BlockSpec(memory_space=pltpu.VMEM)
ANY = pl.BlockSpec(memory_space=pl.ANY)
HBM = pl.BlockSpec(memory_space=pltpu.HBM)
STEP = 2


def blocks(first, last):
    return [(r, min(STEP, last - r)) for r in range(first, last, STEP)]


def rms_silu(values, gain):
    mean_square = jnp.mean(values * values, axis=-1, keepdims=True)
    u = values * lax.rsqrt(mean_square + 1e-06) * (0.5 * gain)
    return u + u * jnp.tanh(u)


def norm_into(shifted, place, row, gain):
    row, scale = row if isinstance(row, tuple) else (row, None)
    normed = rms_silu(row.astype(F32), gain)
    normed = normed if scale is None else normed * scale
    cols = normed.shape[0]
    column = lax.broadcasted_iota(jnp.int32, normed.shape, 0)
    before = jnp.where(column == 0, 0.0, pltpu.roll(normed, 1, 0))
    after = jnp.where(column == cols - 1, 0.0, pltpu.roll(normed, cols - 1, 0))
    shifted[0, place] = before.astype(BF16)
    shifted[1, place] = normed.astype(BF16)
    shifted[2, place] = after.astype(BF16)


def conv_rows(shifted, kernel, place, count):
    cols, channels = shifted.shape[2:]
    total = None
    for i in range(3):
        for j in range(3):
            window = shifted[j, place + i : place + i + count].reshape(count * cols, channels)
            product = jnp.dot(window, kernel[i, j], preferred_element_type=F32)
            total = product if total is None else total + product
    return total


def spatial_jobs(get_row, row_blocks, offset, shifted, sums, slot0, kernel, weights, emit, after=None):
    space_gain, space_bias, time_gain = weights
    ready = set()
    jobs = []

    def norm_stage(first, count):
        for r in range(first - 1, first + count + 1):
            if r not in ready:
                ready.add(r)
                norm_into(shifted, r + offset, get_row(r), space_gain[...])

    def conv_stage(slot, first, count):
        total = conv_rows(shifted, kernel, first - 1 + offset, count)
        sums[slot, : total.shape[0]] = total

    def emit_stage(slot, first, count):
        own = jnp.concatenate([get_row(r) for r in range(first, first + count)], axis=0)
        hidden = own.astype(F32) + sums[slot, : own.shape[0]] + space_bias[...]
        emit(first, count, hidden, rms_silu(hidden, time_gain[...]))

    for n, (first, count) in enumerate(row_blocks):
        slot = (slot0 + n) % sums.shape[0]
        jobs.append([
            functools.partial(norm_stage, first, count),
            functools.partial(conv_stage, slot, first, count),
            functools.partial(emit_stage, slot, first, count),
            functools.partial(after, first, count) if after else None,
        ])
    return jobs


def run(jobs):
    for n in range(len(jobs) + 3):
        for stage in range(4):
            if 0 <= n - stage < len(jobs) and jobs[n - stage][stage] is not None:
                jobs[n - stage][stage]()


def wait_all(pairs, sems):
    copies = [pltpu.make_async_copy(a, b, sems.at[n]) for n, (a, b) in enumerate(pairs)]
    for copy in copies:
        copy.start()
    for copy in copies:
        copy.wait()


def end_pairs(feats, ends):
    rows, lower = feats.shape[1], ends.shape[0] // 2
    upper = ends.shape[0] - lower
    return [
        (feats.at[1, pl.ds(0, upper)], ends.at[pl.ds(0, upper)]),
        (feats.at[1, pl.ds(rows - lower, lower)], ends.at[pl.ds(upper, lower)]),
    ]


def ends_kernel(count, feats, ends, sems):
    first = first_of_pair(count)

    @pl.when(first)
    def _():
        ends[...] = jnp.zeros_like(ends)

    @pl.when(jnp.logical_not(first))
    def _():
        wait_all(end_pairs(feats, ends), sems)


def load_kernel(_, feats, ends, middle, sems):
    upper = ends.shape[0] - ends.shape[0] // 2
    wait_all(end_pairs(feats, ends) + [(feats.at[1, pl.ds(upper, middle.shape[0])], middle)], sems)


def load_rest_kernel(_, feats, kernel, time_kernel, raw_a, kernel_out, time_out, sems):
    wait_all([(feats.at[0], raw_a), (kernel, kernel_out), (time_kernel, time_out)], sems)


def goes_up(index, count):
    return index % 2 == 0 or count % 2 == 1


def halo_ring(frames, bands):
    paired = frames % 2 == 0
    pairs = []
    for f in range(frames):
        for b in range(bands):
            to = (f, b + 1) if goes_up(f, frames) else (f, b - 1)
            if not 0 <= to[1] < bands:
                if not paired:
                    continue
                to = (f ^ 1, b)
            pairs.append((f * bands + b, to[0] * bands + to[1]))
    return pairs


def up_first(count):
    index = lax.axis_index("frame")
    return lax.rem(index, 2) == 0 if count % 2 == 0 else index >= 0


def first_of_pair(count):
    index = lax.axis_index("frame")
    return lax.rem(index, 2) == 0 if count % 2 == 0 else index < 0


def halo_kernel(count, raw_a, edges_b, *refs):
    *arrived, edges, send_0, send_1 = refs
    rows = raw_a.shape[0]
    if len(arrived) == 1:
        edges[...] = arrived[0][...]
    else:
        first = first_of_pair(count)

        @pl.when(first)
        def _():
            edges[...] = arrived[0][...]

        @pl.when(jnp.logical_not(first))
        def _():
            edges[...] = arrived[1][...]

    last = edges.shape[0] - 1

    def fill(up_rows, down_rows):
        for n, (upper, lower) in enumerate((
            (raw_a.at[0], raw_a.at[rows - 1]), (edges_b.at[0], edges_b.at[last]), (edges.at[0], edges.at[last])
        )):
            up_rows[n] = lower[...]
            down_rows[n] = upper[...]

    up = up_first(count)
    pl.when(up)(lambda: fill(send_0, send_1))
    pl.when(jnp.logical_not(up))(lambda: fill(send_1, send_0))


def halo_row(counts, got_0, got_1, n, is_above):
    frames, bands = counts
    band = lax.axis_index("band")
    take = up_first(frames) if is_above else jnp.logical_not(up_first(frames))
    row = jnp.where(take, got_0[n].astype(F32), got_1[n].astype(F32))
    there = band > 0 if is_above else band < bands - 1
    return row, jnp.where(there, 1.0, 0.0)


def framed(upper, ends, middle, lower):
    lower_ends, count = ends.shape[0] // 2, middle.shape[0]
    upper_ends = ends.shape[0] - lower_ends
    rows = ends.shape[0] + count

    def get_row(r):
        if r < 0 or r >= rows:
            return upper() if r < 0 else lower()
        if r < upper_ends or r >= rows - lower_ends:
            return ends[r if r < upper_ends else r - count]
        return middle[r - upper_ends]

    return get_row


def inner_emit(hidden_ref, normed_ref):
    def emit(first, count, hidden, normed):
        at = pl.ds(first - 1, count)
        shape = (count,) + hidden_ref.shape[1:]
        hidden_ref[at] = hidden.astype(hidden_ref.dtype).reshape(shape)
        normed_ref[at] = normed.astype(BF16).reshape(shape)
    return emit


def edge_emit(hidden_ref, normed_ref):
    def emit(first, count, hidden, normed):
        which = 0 if first == 0 else 1
        hidden_ref[which] = hidden
        normed_ref[which] = normed.astype(BF16)
    return emit


def inner_kernel(_, *refs):
    *raw, kernel, space_gain, space_bias, time_gain, hidden_ref, normed_ref, shifted, sums = refs
    get_row = framed(None, *raw, None) if len(raw) == 2 else lambda r: raw[0][r]
    run(spatial_jobs(get_row, blocks(1, hidden_ref.shape[0] + 1), 0, shifted, sums, 0, kernel,
                     (space_gain, space_bias, time_gain), inner_emit(hidden_ref, normed_ref)))


def edges_kernel(counts, raw_a, edges_b, inners_b, got_0, got_1, kernel, space_gain, space_bias, time_gain,
                 time_kernel, hidden_a, normed_a, hidden_b, normed_b, product_a, shifted, sums):
    rows = raw_a.shape[0]
    weights = (space_gain, space_bias, time_gain)

    halo = functools.partial(halo_row, counts, got_0, got_1)

    def row_a(r):
        return halo(0, r < 0) if r < 0 or r >= rows else raw_a[r]

    row_b = framed(lambda: halo(1, True), edges_b, inners_b, lambda: halo(1, False))
    jobs = []
    for n, (get_row, emit) in enumerate((
        (row_a, edge_emit(hidden_a, normed_a)), (row_b, edge_emit(hidden_b, normed_b))
    )):
        for m, (r, offset) in enumerate(((0, 1), (rows - 1, 2 - rows))):
            jobs += spatial_jobs(get_row, [(r, 1)], offset, shifted.at[2 * n + m], sums, 2 * n + m,
                                 kernel, weights, emit)
    run(jobs)
    product = jnp.dot(normed_a[...].reshape(-1, normed_a.shape[-1]), time_kernel[2],
                      preferred_element_type=F32)
    product_a[...] = product.astype(BF16).reshape(product_a.shape)


def main_kernel(counts, edges, inners, got_0, got_1, kernel, space_gain, space_bias, time_gain,
                time_kernel, time_bias, hidden_ae, hidden_ai, normed_ae, normed_ai,
                hidden_be, hidden_bi, normed_be, normed_bi,
                out_ref, base, shifted, sums, normed_p, decoded, sems):
    rows, cols, channels = base.shape
    keep = jnp.where(lax.axis_index("frame") > 0, 1.0, 0.0)

    def emit(first, count, hidden, normed):
        normed_p[first : first + count] = (normed * keep).astype(BF16).reshape(count, cols, channels)

    def rows_of(first, count, *parts):
        get_row = framed(None, *parts, None)
        return jnp.concatenate([get_row(r) for r in range(first, first + count)], axis=0)

    def out_rows(first, count):
        prior = normed_p[first : first + count].reshape(count * cols, channels)
        total = rows_of(first, count, hidden_be, hidden_bi) + time_bias[...]
        total += (
            jnp.dot(rows_of(first, count, normed_be, normed_bi), time_kernel[0], preferred_element_type=F32)
            + jnp.dot(rows_of(first, count, normed_ae, normed_ai), time_kernel[1], preferred_element_type=F32)
            + jnp.dot(prior, time_kernel[2], preferred_element_type=F32)
        )
        decoded[first : first + count] = total.astype(BF16).reshape(count, cols, channels)

    def base_rows(first, count):
        prior = normed_p[first : first + count].reshape(count * cols, channels)
        total = rows_of(first, count, hidden_ae, hidden_ai) + time_bias[...]
        total += (
            jnp.dot(rows_of(first, count, normed_ae, normed_ai), time_kernel[0], preferred_element_type=F32)
            + jnp.dot(prior, time_kernel[1], preferred_element_type=F32)
        )
        base[first : first + count] = total.reshape(count, cols, channels)

    halo = functools.partial(halo_row, counts, got_0, got_1, 2)
    get_row = framed(lambda: halo(True), edges, inners, lambda: halo(False))
    run(spatial_jobs(get_row, blocks(0, rows), 1, shifted, sums, 0, kernel,
                     (space_gain, space_bias, time_gain), emit))
    copies = []
    for n, (first, count) in enumerate(blocks(0, rows)):
        out_rows(first, count)
        copies.append(pltpu.make_async_copy(
            decoded.at[pl.ds(first, count)], out_ref.at[1, pl.ds(first, count)], sems.at[n]))
        copies[-1].start()
    for first, count in blocks(0, rows):
        base_rows(first, count)
    for copy in copies:
        copy.wait()


def inner_finish_kernel(arrived, base, time_kernel, _, out_ref, decoded, sems):
    cols, channels = base.shape[1:]
    keep = jnp.where(lax.axis_index("frame") > 0, 1.0, 0.0)
    kernel = (time_kernel[2].astype(F32) * keep).astype(BF16)
    copies = []
    for n, (row, count) in enumerate(blocks(1, arrived.shape[0] + 1)):
        at = pl.ds(row - 1, count)
        total = base[row : row + count].reshape(count * cols, channels)
        total += jnp.dot(arrived[at].reshape(count * cols, channels), kernel, preferred_element_type=F32)
        decoded[at] = total.astype(BF16).reshape(count, cols, channels)
        copies.append(pltpu.make_async_copy(decoded.at[at], out_ref.at[0, pl.ds(row, count)], sems.at[n]))
        copies[-1].start()
    for copy in copies:
        copy.wait()


def edge_finish_kernel(products, base, _, out_ref, decoded, sems):
    rows = base.shape[0]
    keep = jnp.where(lax.axis_index("frame") > 0, 1.0, 0.0)
    copies = []
    for n, row in enumerate((0, rows - 1)):
        decoded[n] = (base[row] + products[n].astype(F32) * keep).astype(BF16)
        copies.append(pltpu.make_async_copy(decoded.at[pl.ds(n, 1)], out_ref.at[0, pl.ds(row, 1)], sems.at[n]))
        copies[-1].start()
    for copy in copies:
        copy.wait()


def cost(pixels, taps, channels, arrays):
    return pl.CostEstimate(
        flops=2 * pixels * taps * channels * channels,
        bytes_accessed=2 * arrays * pixels * channels,
        transcendentals=2 * pixels * channels,
    )


def body(features, space_kernel, space_gain, space_bias, time_kernel, time_gain, time_bias):
    frames, rows, cols, channels = features.shape
    row = (cols, channels)
    count_f, count_b = lax.axis_size("frame"), lax.axis_size("band")
    counts = (count_f, count_b)
    onward = [(i, (i + 1) % count_f) for i in range(count_f)]
    ring = halo_ring(count_f, count_b)

    def shape(*lead, dtype=BF16):
        return jax.ShapeDtypeStruct(tuple(lead) + row, dtype)

    def room(*lead, dtype=BF16):
        return pltpu.VMEM(tuple(lead) + row, dtype)

    space_gain = space_gain.reshape(1, channels)
    time_gain = time_gain.reshape(1, channels)
    space_bias = space_bias.reshape(1, channels)
    time_bias = time_bias.reshape(1, channels)
    sums = pltpu.VMEM((4, STEP * cols, channels), F32)

    weights = (space_gain, space_bias, time_gain)
    count = len(blocks(0, rows))

    def call(kernel, inputs, outs, scratch, mebibytes, name, **more):
        inputs = [x if isinstance(x, tuple) else (VMEM, x) for x in inputs]
        specs, arrays = zip(*inputs)
        out_specs, out_shape = zip(*((VMEM, o) if not isinstance(o, tuple) else o for o in outs))
        arrays = [x if x.ndim < 3 or s is ANY else pltpu.with_memory_space_constraint(x, s.memory_space)
                  for s, x in zip(specs, arrays)]
        out_shape = [pltpu.VMEM(o.shape, o.dtype) if s is VMEM else o for s, o in zip(out_specs, out_shape)]
        return pl.pallas_call(
            kernel, in_specs=list(specs), out_specs=list(out_specs), out_shape=out_shape,
            scratch_shapes=scratch, name=name,
            compiler_params=pltpu.CompilerParams(vmem_limit_bytes=mebibytes * 1024 * 1024), **more,
        )(*arrays)

    def inner_rows(raw, scale, name, after):
        return call(
            inner_kernel, [(ANY, after), *raw, space_kernel, *weights],
            [shape(rows - 2, dtype=F32), shape(rows - 2)], [room(3, rows), sums],
            6, name, cost_estimate=cost(rows * cols, 9 * scale, channels, 3),
        )

    held = 3 if rows >= 6 else 2
    (ends,) = call(
        functools.partial(ends_kernel, count_f), [(HBM, features)], [shape(held)],
        [pltpu.SemaphoreType.DMA((2,))], 1, "ends",
    )
    edge = [lax.ppermute(ends, "frame", onward)]
    edge_out, inner_out = call(
        load_kernel, [(ANY, ends), (HBM, features)], [shape(held), shape(rows - held)],
        [pltpu.SemaphoreType.DMA((3,))], 1, "load",
    )
    raw_a, space_kernel, time_kernel = call(
        load_rest_kernel, [(ANY, inner_out), (HBM, features), (HBM, space_kernel), (HBM, time_kernel)],
        [shape(rows), jax.ShapeDtypeStruct(space_kernel.shape, BF16),
         jax.ShapeDtypeStruct(time_kernel.shape, BF16)],
        [pltpu.SemaphoreType.DMA((3,))], 1, "load_rest",
    )
    inner = lax.ppermute(inner_out, "frame", onward)
    if count_f % 2 == 0:
        edge.append(lax.ppermute(edge_out, "frame", [(f, f ^ 1) for f in range(count_f)]))

    edge, send_0, send_1 = call(
        functools.partial(halo_kernel, count_f), [raw_a, edge_out, *edge],
        [shape(held), shape(3), shape(3)], [], 1, "halo",
    )
    hidden_ai, normed_ai = inner_rows([raw_a], 8, "inner_a", send_0)
    got_0 = lax.ppermute(send_0, ("frame", "band"), ring)
    got_1 = lax.ppermute(send_1, ("frame", "band"), [(t, s) for s, t in ring])
    arrived = lax.ppermute(normed_ai, "frame", onward[:-1])
    hidden_bi, normed_bi = inner_rows([edge_out, inner_out], 1, "inner_b", normed_ai)
    hidden_ae, normed_ae, hidden_be, normed_be, product_ae = call(
        functools.partial(edges_kernel, counts), [raw_a, edge_out, inner_out, got_0, got_1, space_kernel, *weights,
         time_kernel],
        [shape(2, dtype=F32), shape(2)] * 2 + [shape(2)], [room(4, 3, 3), sums],
        4, "edges", cost_estimate=cost(4 * cols, 9, channels, 3),
    )
    edge_arrived = lax.ppermute(product_ae, "frame", onward)

    decoded, base = call(
        functools.partial(main_kernel, counts),
        [edge, inner, got_0, got_1, space_kernel, *weights, time_kernel, time_bias,
         hidden_ae, hidden_ai, normed_ae, normed_ai, hidden_be, hidden_bi, normed_be, normed_bi],
        [(ANY, jax.ShapeDtypeStruct(features.shape, BF16)), shape(rows, dtype=F32)],
        [room(3, rows + 2), sums, room(rows), room(rows), pltpu.SemaphoreType.DMA((count,))],
        9, "main", cost_estimate=cost(rows * cols, 14 * 8, channels, 10),
    )
    for kernel, inputs, n in (
        (inner_finish_kernel, [arrived, base, time_kernel], len(blocks(1, rows - 1))),
        (edge_finish_kernel, [edge_arrived, base], 2),
    ):
        (decoded,) = call(
            kernel, [*inputs, (ANY, decoded)], [(ANY, jax.ShapeDtypeStruct(features.shape, BF16))],
            [room(inputs[0].shape[0]), pltpu.SemaphoreType.DMA((n,))],
            3, "finish", input_output_aliases={len(inputs): 0},
            cost_estimate=cost(inputs[0].shape[0] * cols, 1, channels, 4),
        )
    return decoded


def solution(mesh):
    return jax.shard_map(
        body,
        mesh=mesh,
        in_specs=(P(("grp", "frame"), "band", None, None), P(), P(), P(), P(), P(), P()),
        out_specs=P(("grp", "frame"), "band", None, None),
        check_vma=False,
    )
```

```python
import functools

import jax
import jax.numpy as jnp
from jax import lax
from jax.experimental import pallas as pl
from jax.experimental.pallas import tpu as pltpu
from jax.sharding import PartitionSpec as P

F32 = jnp.float32
BF16 = jnp.bfloat16
VMEM = pl.BlockSpec(memory_space=pltpu.VMEM)
ANY = pl.BlockSpec(memory_space=pl.ANY)
HBM = pl.BlockSpec(memory_space=pltpu.HBM)
STEP = 2
RING_ROWS = 4


def blocks(first, last):
    return [(r, min(STEP, last - r)) for r in range(first, last, STEP)]


def rms_silu(values, gain):
    mean_square = jnp.mean(values * values, axis=-1, keepdims=True)
    u = values * lax.rsqrt(mean_square + 1e-06) * (0.5 * gain)
    return u + u * jnp.tanh(u)


def norm_into(shifted, place, row, gain):
    row, scale = row if isinstance(row, tuple) else (row, None)
    normed = rms_silu(row.astype(F32), gain)
    normed = normed if scale is None else normed * scale
    cols = normed.shape[0]
    column = lax.broadcasted_iota(jnp.int32, normed.shape, 0)
    before = jnp.where(column == 0, 0.0, pltpu.roll(normed, 1, 0))
    after = jnp.where(column == cols - 1, 0.0, pltpu.roll(normed, cols - 1, 0))
    shifted[0, place] = before.astype(BF16)
    shifted[1, place] = normed.astype(BF16)
    shifted[2, place] = after.astype(BF16)


def conv_rows(shifted, kernel, place, count):
    cols, channels = shifted.shape[2:]
    total = None
    for i in range(3):
        for j in range(3):
            window = shifted[j, place + i : place + i + count].reshape(count * cols, channels)
            product = jnp.dot(window, kernel[i, j], preferred_element_type=F32)
            total = product if total is None else total + product
    return total


def spatial_jobs(get_row, row_blocks, offset, shifted, sums, slot0, kernel, weights, emit, after=None):
    space_gain, space_bias, time_gain = weights
    ready = set()
    jobs = []

    def norm_stage(first, count):
        for r in range(first - 1, first + count + 1):
            if r not in ready:
                ready.add(r)
                norm_into(shifted, r + offset, get_row(r), space_gain[...])

    def conv_stage(slot, first, count):
        total = conv_rows(shifted, kernel, first - 1 + offset, count)
        sums[slot, : total.shape[0]] = total

    def emit_stage(slot, first, count):
        own = jnp.concatenate([get_row(r) for r in range(first, first + count)], axis=0)
        hidden = own.astype(F32) + sums[slot, : own.shape[0]] + space_bias[...]
        emit(first, count, hidden, rms_silu(hidden, time_gain[...]))

    for n, (first, count) in enumerate(row_blocks):
        slot = (slot0 + n) % sums.shape[0]
        jobs.append([
            functools.partial(norm_stage, first, count),
            functools.partial(conv_stage, slot, first, count),
            functools.partial(emit_stage, slot, first, count),
            functools.partial(after, first, count) if after else None,
        ])
    return jobs


def run(jobs):
    for n in range(len(jobs) + 3):
        for stage in range(4):
            if 0 <= n - stage < len(jobs) and jobs[n - stage][stage] is not None:
                jobs[n - stage][stage]()


def wait_all(pairs, sems):
    copies = [pltpu.make_async_copy(a, b, sems.at[n]) for n, (a, b) in enumerate(pairs)]
    for copy in copies:
        copy.start()
    for copy in copies:
        copy.wait()


def end_pairs(feats, ends):
    rows, lower = feats.shape[1], ends.shape[0] // 2
    upper = ends.shape[0] - lower
    return [
        (feats.at[1, pl.ds(0, upper)], ends.at[pl.ds(0, upper)]),
        (feats.at[1, pl.ds(rows - lower, lower)], ends.at[pl.ds(upper, lower)]),
    ]


def ends_kernel(count, feats, ends, sems):
    first = first_of_pair(count)

    @pl.when(first)
    def _():
        ends[...] = jnp.zeros_like(ends)

    @pl.when(jnp.logical_not(first))
    def _():
        wait_all(end_pairs(feats, ends), sems)


def load_kernel(_, feats, ends, middle, sems):
    upper = ends.shape[0] - ends.shape[0] // 2
    wait_all(end_pairs(feats, ends) + [(feats.at[1, pl.ds(upper, middle.shape[0])], middle)], sems)


def load_rest_kernel(_, feats, kernel, time_kernel, raw_a, kernel_out, time_out, sems):
    wait_all([(feats.at[0], raw_a), (kernel, kernel_out), (time_kernel, time_out)], sems)


def goes_up(index, count):
    return index % 2 == 0 or count % 2 == 1


def halo_ring(frames, bands):
    paired = frames % 2 == 0
    pairs = []
    for f in range(frames):
        for b in range(bands):
            to = (f, b + 1) if goes_up(f, frames) else (f, b - 1)
            if not 0 <= to[1] < bands:
                if not paired:
                    continue
                to = (f ^ 1, b)
            pairs.append((f * bands + b, to[0] * bands + to[1]))
    return pairs


def up_first(count):
    index = lax.axis_index("frame")
    return lax.rem(index, 2) == 0 if count % 2 == 0 else index >= 0


def first_of_pair(count):
    index = lax.axis_index("frame")
    return lax.rem(index, 2) == 0 if count % 2 == 0 else index < 0


def copy_kernel(source, target):
    target[...] = source[...]


def halo_kernel(count, raw_a, edges_b, *refs):
    *arrived, edges, send_0, send_1 = refs
    rows = raw_a.shape[0]
    if len(arrived) == 1:
        edges[...] = arrived[0][...]
    else:
        first = first_of_pair(count)

        @pl.when(first)
        def _():
            edges[...] = arrived[0][...]

        @pl.when(jnp.logical_not(first))
        def _():
            edges[...] = arrived[1][...]

    last = edges.shape[0] - 1

    def fill(up_rows, down_rows):
        for n, (upper, lower) in enumerate((
            (raw_a.at[0], raw_a.at[rows - 1]), (edges_b.at[0], edges_b.at[last]), (edges.at[0], edges.at[last])
        )):
            up_rows[n] = lower[...]
            down_rows[n] = upper[...]

    up = up_first(count)
    pl.when(up)(lambda: fill(send_0, send_1))
    pl.when(jnp.logical_not(up))(lambda: fill(send_1, send_0))


def halo_row(counts, got_0, got_1, n, is_above):
    frames, bands = counts
    band = lax.axis_index("band")
    take = up_first(frames) if is_above else jnp.logical_not(up_first(frames))
    row = jnp.where(take, got_0[n].astype(F32), got_1[n].astype(F32))
    there = band > 0 if is_above else band < bands - 1
    return row, jnp.where(there, 1.0, 0.0)


def framed(upper, ends, middle, lower):
    middle = middle if isinstance(middle, list) else [middle]
    lower_ends, count = ends.shape[0] // 2, sum(part.shape[0] for part in middle)
    upper_ends = ends.shape[0] - lower_ends
    rows = ends.shape[0] + count

    def get_row(r):
        if r < 0 or r >= rows:
            return upper() if r < 0 else lower()
        if r < upper_ends or r >= rows - lower_ends:
            return ends[r if r < upper_ends else r - count]
        part, at = part_of(middle, r - upper_ends)
        return part[at]

    return get_row


def part_of(parts, row):
    for part in parts:
        if row < part.shape[0]:
            return part, row
        row -= part.shape[0]


def inner_emit(start, hidden_ref, normed_ref):
    def emit(first, count, hidden, normed):
        at = pl.ds(first - start, count)
        shape = (count,) + hidden_ref.shape[1:]
        hidden_ref[at] = hidden.astype(hidden_ref.dtype).reshape(shape)
        normed_ref[at] = normed.astype(BF16).reshape(shape)
    return emit


def edge_emit(hidden_ref, normed_ref):
    def emit(first, count, hidden, normed):
        which = 0 if first == 0 else 1
        hidden_ref[which] = hidden
        normed_ref[which] = normed.astype(BF16)
    return emit


def inner_kernel(start, _, *refs):
    *raw, kernel, space_gain, space_bias, time_gain, hidden_ref, normed_ref, shifted, sums = refs
    get_row = framed(None, *raw, None) if len(raw) == 2 else lambda r: raw[0][r]
    run(spatial_jobs(get_row, blocks(start, start + hidden_ref.shape[0]), 1 - start, shifted, sums, 0, kernel,
                     (space_gain, space_bias, time_gain), inner_emit(start, hidden_ref, normed_ref)))


def edges_kernel(counts, raw_a, edges_b, inners_b, got_0, got_1, kernel, space_gain, space_bias, time_gain,
                 time_kernel, hidden_a, normed_a, hidden_b, normed_b, product_a, shifted, sums):
    rows = raw_a.shape[0]
    weights = (space_gain, space_bias, time_gain)

    halo = functools.partial(halo_row, counts, got_0, got_1)

    def row_a(r):
        return halo(0, r < 0) if r < 0 or r >= rows else raw_a[r]

    row_b = framed(lambda: halo(1, True), edges_b, inners_b, lambda: halo(1, False))
    jobs = []
    for n, (get_row, emit) in enumerate((
        (row_a, edge_emit(hidden_a, normed_a)), (row_b, edge_emit(hidden_b, normed_b))
    )):
        for m, (r, offset) in enumerate(((0, 1), (rows - 1, 2 - rows))):
            jobs += spatial_jobs(get_row, [(r, 1)], offset, shifted.at[2 * n + m], sums, 2 * n + m,
                                 kernel, weights, emit)
    run(jobs)
    product = jnp.dot(normed_a[...].reshape(-1, normed_a.shape[-1]), time_kernel[2],
                      preferred_element_type=F32)
    product_a[...] = product.astype(BF16).reshape(product_a.shape)


def main_kernel(counts, ring_start, edges, inners, got_0, got_1, kernel, space_gain, space_bias, time_gain,
                time_kernel, time_bias, hidden_be, hidden_bi, normed_be, normed_bi, hidden_ae, normed_ae, *refs):
    *refs, out_ref, base, shifted, sums, normed_p, decoded, decoded_ring, sems = refs
    inner_a, arrived = (refs[:4], refs[4]) if len(refs) > 4 else (refs, None)
    hidden_ai, normed_ai = inner_a[::2], inner_a[1::2]
    rows, cols, channels = base.shape
    keep = jnp.where(lax.axis_index("frame") > 0, 1.0, 0.0)

    def emit(first, count, hidden, normed):
        normed_p[first : first + count] = (normed * keep).astype(BF16).reshape(count, cols, channels)

    def rows_of(first, count, *parts):
        get_row = framed(None, *parts, None)
        return jnp.concatenate([get_row(r) for r in range(first, first + count)], axis=0)

    def out_rows(first, count):
        prior = normed_p[first : first + count].reshape(count * cols, channels)
        total = rows_of(first, count, hidden_be, hidden_bi) + time_bias[...]
        total += (
            jnp.dot(rows_of(first, count, normed_be, normed_bi), time_kernel[0], preferred_element_type=F32)
            + jnp.dot(rows_of(first, count, normed_ae, normed_ai), time_kernel[1], preferred_element_type=F32)
            + jnp.dot(prior, time_kernel[2], preferred_element_type=F32)
        )
        decoded[first : first + count] = total.astype(BF16).reshape(count, cols, channels)

    def base_rows(first, count):
        prior = normed_p[first : first + count].reshape(count * cols, channels)
        total = rows_of(first, count, hidden_ae, hidden_ai) + time_bias[...]
        total += (
            jnp.dot(rows_of(first, count, normed_ae, normed_ai), time_kernel[0], preferred_element_type=F32)
            + jnp.dot(prior, time_kernel[1], preferred_element_type=F32)
        )
        return total

    halo = functools.partial(halo_row, counts, got_0, got_1, 2)
    get_row = framed(lambda: halo(True), edges, inners, lambda: halo(False))
    run(spatial_jobs(get_row, blocks(0, rows), 1, shifted, sums, 0, kernel,
                     (space_gain, space_bias, time_gain), emit))
    copies = []

    def write(frame, row, held, at):
        copies.append(pltpu.make_async_copy(held.at[at], out_ref.at[frame, row], sems.at[len(copies)]))
        copies[-1].start()

    for first, count in blocks(0, rows):
        out_rows(first, count)
        write(1, pl.ds(first, count), decoded, pl.ds(first, count))
    ring_end = ring_start + (0 if arrived is None else arrived.shape[0])
    lag_kernel = (time_kernel[2].astype(F32) * keep).astype(BF16)
    for first, count in blocks(ring_start, ring_end):
        at = pl.ds(first - ring_start, count)
        total = base_rows(first, count)
        total += jnp.dot(arrived[at].reshape(count * cols, channels), lag_kernel, preferred_element_type=F32)
        decoded_ring[at] = total.astype(BF16).reshape(count, cols, channels)
        write(0, pl.ds(first, count), decoded_ring, at)
    for first, count in blocks(0, ring_start) + blocks(ring_end, rows):
        base[first : first + count] = base_rows(first, count).reshape(count, cols, channels)
    for copy in copies:
        copy.wait()


def waits_at_end(count):
    return jnp.logical_and(first_of_pair(count), lax.axis_index("frame") > 0)


def inner_finish_kernel(frames, arrived, base, time_kernel, _, decoded, out_ref, sems):
    cols, channels = base.shape[1:]
    keep = jnp.where(lax.axis_index("frame") > 0, 1.0, 0.0)
    kernel = (time_kernel[2].astype(F32) * keep).astype(BF16)
    for row, count in blocks(1, arrived.shape[0] + 1):
        at = pl.ds(row - 1, count)
        total = base[row : row + count].reshape(count * cols, channels)
        total += jnp.dot(arrived[at].reshape(count * cols, channels), kernel, preferred_element_type=F32)
        decoded[at] = total.astype(BF16).reshape(count, cols, channels)
    copy = pltpu.make_async_copy(decoded, out_ref.at[0, pl.ds(1, decoded.shape[0])], sems.at[0])

    @pl.when(waits_at_end(frames))
    def _():
        copy.start()
        copy.wait()


def finish_kernel(frames, decoded, products, base, _, out_ref, edges, sems):
    rows, count = base.shape[0], decoded.shape[0]
    keep = jnp.where(lax.axis_index("frame") > 0, 1.0, 0.0)
    second = jnp.logical_not(waits_at_end(frames))
    inner = pltpu.make_async_copy(decoded, out_ref.at[0, pl.ds(1, count)], sems.at[2])
    pl.when(second)(inner.start)
    copies = []
    for n, row in enumerate((0, rows - 1)):
        edges[n] = (base[row] + products[n].astype(F32) * keep).astype(BF16)
        copies.append(pltpu.make_async_copy(edges.at[pl.ds(n, 1)], out_ref.at[0, pl.ds(row, 1)], sems.at[n]))
        copies[-1].start()
    for copy in copies:
        copy.wait()
    pl.when(second)(inner.wait)


def cost(pixels, taps, channels, arrays):
    return pl.CostEstimate(
        flops=2 * pixels * taps * channels * channels,
        bytes_accessed=2 * arrays * pixels * channels,
        transcendentals=2 * pixels * channels,
    )


def body(features, space_kernel, space_gain, space_bias, time_kernel, time_gain, time_bias):
    frames, rows, cols, channels = features.shape
    row = (cols, channels)
    count_f, count_b = lax.axis_size("frame"), lax.axis_size("band")
    counts = (count_f, count_b)
    onward = [(i, (i + 1) % count_f) for i in range(count_f)]
    ring = halo_ring(count_f, count_b)

    def shape(*lead, dtype=BF16):
        return jax.ShapeDtypeStruct(tuple(lead) + row, dtype)

    def room(*lead, dtype=BF16):
        return pltpu.VMEM(tuple(lead) + row, dtype)

    space_gain = space_gain.reshape(1, channels)
    time_gain = time_gain.reshape(1, channels)
    space_bias = space_bias.reshape(1, channels)
    time_bias = time_bias.reshape(1, channels)
    sums = pltpu.VMEM((4, STEP * cols, channels), F32)

    weights = (space_gain, space_bias, time_gain)
    count = len(blocks(0, rows))

    def call(kernel, inputs, outs, scratch, mebibytes, name, **more):
        inputs = [x if isinstance(x, tuple) else (VMEM, x) for x in inputs]
        specs, arrays = zip(*inputs)
        out_specs, out_shape = zip(*((VMEM, o) if not isinstance(o, tuple) else o for o in outs))
        arrays = [x if x.ndim < 3 or s is ANY else pltpu.with_memory_space_constraint(x, s.memory_space)
                  for s, x in zip(specs, arrays)]
        out_shape = [pltpu.VMEM(o.shape, o.dtype) if s is VMEM else o for s, o in zip(out_specs, out_shape)]
        return pl.pallas_call(
            kernel, in_specs=list(specs), out_specs=list(out_specs), out_shape=out_shape,
            scratch_shapes=scratch, name=name,
            compiler_params=pltpu.CompilerParams(vmem_limit_bytes=mebibytes * 1024 * 1024), **more,
        )(*arrays)

    def inner_rows(raw, start, n, scale, name, after):
        return call(
            functools.partial(inner_kernel, start), [(ANY, after), *raw, space_kernel, *weights],
            [shape(n, dtype=F32), shape(n)], [room(3, n + 2), sums],
            6, name, cost_estimate=cost(n * cols, 9 * scale, channels, 3),
        )

    held = 3 if rows >= 6 else 2
    (ends,) = call(
        functools.partial(ends_kernel, count_f), [(HBM, features)], [shape(held)],
        [pltpu.SemaphoreType.DMA((2,))], 1, "ends",
    )
    edge = [lax.ppermute(ends, "frame", onward)]
    edge_out, inner_out = call(
        load_kernel, [(ANY, ends), (HBM, features)], [shape(held), shape(rows - held)],
        [pltpu.SemaphoreType.DMA((3,))], 1, "load",
    )
    raw_a, space_kernel, time_kernel = call(
        load_rest_kernel, [(ANY, inner_out), (HBM, features), (HBM, space_kernel), (HBM, time_kernel)],
        [shape(rows), jax.ShapeDtypeStruct(space_kernel.shape, BF16),
         jax.ShapeDtypeStruct(time_kernel.shape, BF16)],
        [pltpu.SemaphoreType.DMA((3,))], 1, "load_rest",
    )
    inner = lax.ppermute(inner_out, "frame", onward)
    if count_f % 2 == 0:
        edge.append(lax.ppermute(edge_out, "frame", [(f, f ^ 1) for f in range(count_f)]))

    ring_rows = min(RING_ROWS, (rows - 2) // STEP // 2 * STEP)
    parts = [rows - 2 - ring_rows] + [ring_rows] * (ring_rows > 0)
    inner_a = []
    if ring_rows:
        inner_a = inner_rows([raw_a], 1 + parts[0], ring_rows, 1, "inner_a_ring", raw_a)
    (edge[0],) = call(copy_kernel, [edge[0]], [shape(held)], [], 1, "arrived")
    edge, send_0, send_1 = call(
        functools.partial(halo_kernel, count_f), [raw_a, edge_out, *edge],
        [shape(held), shape(3), shape(3)], [], 1, "halo",
    )
    inner_a = [*inner_rows([raw_a], 1, parts[0], 8, "inner_a", send_0), *inner_a]
    normed_ai = inner_a[1::2]
    got_0 = lax.ppermute(send_0, ("frame", "band"), ring)
    got_1 = lax.ppermute(send_1, ("frame", "band"), [(t, s) for s, t in ring])
    arrived = [lax.ppermute(normed_ai[0], "frame", onward[:-1])]
    arrived += [lax.ppermute(part, "frame", onward) for part in normed_ai[1:]]
    hidden_bi, normed_bi = inner_rows([edge_out, inner_out], 1, rows - 2, 1, "inner_b", normed_ai[0])
    hidden_ae, normed_ae, hidden_be, normed_be, product_ae = call(
        functools.partial(edges_kernel, counts), [raw_a, edge_out, inner_out, got_0, got_1, space_kernel, *weights,
         time_kernel],
        [shape(2, dtype=F32), shape(2)] * 2 + [shape(2)], [room(4, 3, 3), sums],
        4, "edges", cost_estimate=cost(4 * cols, 9, channels, 3),
    )
    edge_arrived = lax.ppermute(product_ae, "frame", onward)

    decoded, base = call(
        functools.partial(main_kernel, counts, 1 + parts[0]),
        [edge, inner, got_0, got_1, space_kernel, *weights, time_kernel, time_bias,
         hidden_be, hidden_bi, normed_be, normed_bi, hidden_ae, normed_ae, *inner_a, *arrived[1:]],
        [(ANY, jax.ShapeDtypeStruct(features.shape, BF16)), shape(rows, dtype=F32)],
        [room(3, rows + 2), sums, room(rows), room(rows), room(max(ring_rows, 1)),
         pltpu.SemaphoreType.DMA((2 * count,))],
        9, "main", cost_estimate=cost(rows * cols, 14 * 8, channels, 10),
    )
    decoded_a, decoded = call(
        functools.partial(inner_finish_kernel, count_f), [arrived[0], base, time_kernel, (ANY, decoded)],
        [shape(parts[0]), (ANY, jax.ShapeDtypeStruct(features.shape, BF16))], [pltpu.SemaphoreType.DMA((1,))],
        3, "inner_finish", input_output_aliases={3: 1}, cost_estimate=cost(parts[0] * cols, 1, channels, 4),
    )
    (decoded,) = call(
        functools.partial(finish_kernel, count_f), [decoded_a, edge_arrived, base, (ANY, decoded)],
        [(ANY, jax.ShapeDtypeStruct(features.shape, BF16))], [room(2), pltpu.SemaphoreType.DMA((3,))],
        3, "finish", input_output_aliases={3: 0}, cost_estimate=cost(2 * cols, 1, channels, 4),
    )
    return decoded


def solution(mesh):
    return jax.shard_map(
        body,
        mesh=mesh,
        in_specs=(P(("grp", "frame"), "band", None, None), P(), P(), P(), P(), P(), P()),
        out_specs=P(("grp", "frame"), "band", None, None),
        check_vma=False,
    )
```

```python
import functools

import jax
import jax.numpy as jnp
from jax import lax
from jax.experimental import pallas as pl
from jax.experimental.pallas import tpu as pltpu
from jax.sharding import PartitionSpec as P

F32 = jnp.float32
BF16 = jnp.bfloat16
VMEM = pl.BlockSpec(memory_space=pltpu.VMEM)
ANY = pl.BlockSpec(memory_space=pl.ANY)
HBM = pl.BlockSpec(memory_space=pltpu.HBM)
STEP = 2
RING_ROWS = 6


def blocks(first, last):
    return [(r, min(STEP, last - r)) for r in range(first, last, STEP)]


def rms_silu(values, gain):
    mean_square = jnp.mean(values * values, axis=-1, keepdims=True)
    u = values * lax.rsqrt(mean_square + 1e-06) * (0.5 * gain)
    return u + u * jnp.tanh(u)


def norm_into(shifted, place, row, gain):
    row, scale = row if isinstance(row, tuple) else (row, None)
    normed = rms_silu(row.astype(F32), gain)
    normed = normed if scale is None else normed * scale
    cols = normed.shape[0]
    column = lax.broadcasted_iota(jnp.int32, normed.shape, 0)
    before = jnp.where(column == 0, 0.0, pltpu.roll(normed, 1, 0))
    after = jnp.where(column == cols - 1, 0.0, pltpu.roll(normed, cols - 1, 0))
    shifted[0, place] = before.astype(BF16)
    shifted[1, place] = normed.astype(BF16)
    shifted[2, place] = after.astype(BF16)


def conv_rows(shifted, kernel, place, count):
    cols, channels = shifted.shape[2:]
    total = None
    for i in range(3):
        for j in range(3):
            window = shifted[j, place + i : place + i + count].reshape(count * cols, channels)
            product = jnp.dot(window, kernel[i, j], preferred_element_type=F32)
            total = product if total is None else total + product
    return total


def spatial_jobs(get_row, row_blocks, offset, shifted, sums, slot0, kernel, weights, emit, after=None):
    space_gain, space_bias, time_gain = weights
    ready = set()
    jobs = []

    def norm_stage(first, count):
        for r in range(first - 1, first + count + 1):
            if r not in ready:
                ready.add(r)
                norm_into(shifted, r + offset, get_row(r), space_gain[...])

    def conv_stage(slot, first, count):
        total = conv_rows(shifted, kernel, first - 1 + offset, count)
        sums[slot, : total.shape[0]] = total

    def emit_stage(slot, first, count):
        own = jnp.concatenate([get_row(r) for r in range(first, first + count)], axis=0)
        hidden = own.astype(F32) + sums[slot, : own.shape[0]] + space_bias[...]
        emit(first, count, hidden, rms_silu(hidden, time_gain[...]))

    for n, (first, count) in enumerate(row_blocks):
        slot = (slot0 + n) % sums.shape[0]
        jobs.append([
            functools.partial(norm_stage, first, count),
            functools.partial(conv_stage, slot, first, count),
            functools.partial(emit_stage, slot, first, count),
            functools.partial(after, first, count) if after else None,
        ])
    return jobs


def run(jobs):
    for n in range(len(jobs) + 3):
        for stage in range(4):
            if 0 <= n - stage < len(jobs) and jobs[n - stage][stage] is not None:
                jobs[n - stage][stage]()


def wait_all(pairs, sems):
    copies = [pltpu.make_async_copy(a, b, sems.at[n]) for n, (a, b) in enumerate(pairs)]
    for copy in copies:
        copy.start()
    for copy in copies:
        copy.wait()


def end_pairs(feats, ends):
    rows, lower = feats.shape[1], ends.shape[0] // 2
    upper = ends.shape[0] - lower
    return [
        (feats.at[1, pl.ds(0, upper)], ends.at[pl.ds(0, upper)]),
        (feats.at[1, pl.ds(rows - lower, lower)], ends.at[pl.ds(upper, lower)]),
    ]


def ends_kernel(count, feats, ends, sems):
    first = first_of_pair(count)

    @pl.when(first)
    def _():
        ends[...] = jnp.zeros_like(ends)

    @pl.when(jnp.logical_not(first))
    def _():
        wait_all(end_pairs(feats, ends), sems)


def load_kernel(_, feats, ends, middle, sems):
    upper = ends.shape[0] - ends.shape[0] // 2
    wait_all(end_pairs(feats, ends) + [(feats.at[1, pl.ds(upper, middle.shape[0])], middle)], sems)


def load_rest_kernel(_, feats, kernel, time_kernel, raw_a, kernel_out, time_out, sems):
    wait_all([(feats.at[0], raw_a), (kernel, kernel_out), (time_kernel, time_out)], sems)


def goes_up(index, count):
    return index % 2 == 0 or count % 2 == 1


def halo_ring(frames, bands):
    paired = frames % 2 == 0
    pairs = []
    for f in range(frames):
        for b in range(bands):
            to = (f, b + 1) if goes_up(f, frames) else (f, b - 1)
            if not 0 <= to[1] < bands:
                if not paired:
                    continue
                to = (f ^ 1, b)
            pairs.append((f * bands + b, to[0] * bands + to[1]))
    return pairs


def up_first(count):
    index = lax.axis_index("frame")
    return lax.rem(index, 2) == 0 if count % 2 == 0 else index >= 0


def first_of_pair(count):
    index = lax.axis_index("frame")
    return lax.rem(index, 2) == 0 if count % 2 == 0 else index < 0


def copy_kernel(source, target):
    target[...] = source[...]


def halo_kernel(count, raw_a, edges_b, *refs):
    *arrived, edges, send_0, send_1 = refs
    rows = raw_a.shape[0]
    if len(arrived) == 1:
        edges[...] = arrived[0][...]
    else:
        first = first_of_pair(count)

        @pl.when(first)
        def _():
            edges[...] = arrived[0][...]

        @pl.when(jnp.logical_not(first))
        def _():
            edges[...] = arrived[1][...]

    last = edges.shape[0] - 1

    def fill(up_rows, down_rows):
        for n, (upper, lower) in enumerate((
            (raw_a.at[0], raw_a.at[rows - 1]), (edges_b.at[0], edges_b.at[last]), (edges.at[0], edges.at[last])
        )):
            up_rows[n] = lower[...]
            down_rows[n] = upper[...]

    up = up_first(count)
    pl.when(up)(lambda: fill(send_0, send_1))
    pl.when(jnp.logical_not(up))(lambda: fill(send_1, send_0))


def halo_row(counts, got_0, got_1, n, is_above):
    frames, bands = counts
    band = lax.axis_index("band")
    take = up_first(frames) if is_above else jnp.logical_not(up_first(frames))
    row = jnp.where(take, got_0[n].astype(F32), got_1[n].astype(F32))
    there = band > 0 if is_above else band < bands - 1
    return row, jnp.where(there, 1.0, 0.0)


def framed(upper, ends, middle, lower):
    middle = middle if isinstance(middle, list) else [middle]
    lower_ends, count = ends.shape[0] // 2, sum(part.shape[0] for part in middle)
    upper_ends = ends.shape[0] - lower_ends
    rows = ends.shape[0] + count

    def get_row(r):
        if r < 0 or r >= rows:
            return upper() if r < 0 else lower()
        if r < upper_ends or r >= rows - lower_ends:
            return ends[r if r < upper_ends else r - count]
        part, at = part_of(middle, r - upper_ends)
        return part[at]

    return get_row


def part_of(parts, row):
    for part in parts:
        if row < part.shape[0]:
            return part, row
        row -= part.shape[0]


def inner_emit(start, hidden_ref, normed_ref):
    def emit(first, count, hidden, normed):
        at = pl.ds(first - start, count)
        shape = (count,) + hidden_ref.shape[1:]
        hidden_ref[at] = hidden.astype(hidden_ref.dtype).reshape(shape)
        normed_ref[at] = normed.astype(BF16).reshape(shape)
    return emit


def edge_emit(hidden_ref, normed_ref):
    def emit(first, count, hidden, normed):
        which = 0 if first == 0 else 1
        hidden_ref[which] = hidden
        normed_ref[which] = normed.astype(BF16)
    return emit


def inner_kernel(start, _, *refs):
    *raw, kernel, space_gain, space_bias, time_gain, hidden_ref, normed_ref, shifted, sums = refs
    get_row = framed(None, *raw, None) if len(raw) == 2 else lambda r: raw[0][r]
    run(spatial_jobs(get_row, blocks(start, start + hidden_ref.shape[0]), 1 - start, shifted, sums, 0, kernel,
                     (space_gain, space_bias, time_gain), inner_emit(start, hidden_ref, normed_ref)))


def edges_kernel(counts, raw_a, edges_b, inners_b, got_0, got_1, kernel, space_gain, space_bias, time_gain,
                 time_kernel, hidden_a, normed_a, hidden_b, normed_b, product_a, shifted, sums):
    rows = raw_a.shape[0]
    weights = (space_gain, space_bias, time_gain)

    halo = functools.partial(halo_row, counts, got_0, got_1)

    def row_a(r):
        return halo(0, r < 0) if r < 0 or r >= rows else raw_a[r]

    row_b = framed(lambda: halo(1, True), edges_b, inners_b, lambda: halo(1, False))
    jobs = []
    for n, (get_row, emit) in enumerate((
        (row_a, edge_emit(hidden_a, normed_a)), (row_b, edge_emit(hidden_b, normed_b))
    )):
        for m, (r, offset) in enumerate(((0, 1), (rows - 1, 2 - rows))):
            jobs += spatial_jobs(get_row, [(r, 1)], offset, shifted.at[2 * n + m], sums, 2 * n + m,
                                 kernel, weights, emit)
    run(jobs)
    product = jnp.dot(normed_a[...].reshape(-1, normed_a.shape[-1]), time_kernel[2],
                      preferred_element_type=F32)
    product_a[...] = product.astype(BF16).reshape(product_a.shape)


def main_kernel(counts, edges, inners, got_0, got_1, kernel, space_gain, space_bias, time_gain,
                time_kernel, time_bias, hidden_be, hidden_bi, normed_be, normed_bi, hidden_ae, normed_ae, *refs):
    *inner_a, out_ref, base, shifted, sums, normed_p, decoded, sems = refs
    hidden_ai, normed_ai = inner_a[::2], inner_a[1::2]
    rows, cols, channels = base.shape
    keep = jnp.where(lax.axis_index("frame") > 0, 1.0, 0.0)

    def emit(first, count, hidden, normed):
        normed_p[first : first + count] = (normed * keep).astype(BF16).reshape(count, cols, channels)

    def rows_of(first, count, *parts):
        get_row = framed(None, *parts, None)
        return jnp.concatenate([get_row(r) for r in range(first, first + count)], axis=0)

    def out_rows(first, count):
        prior = normed_p[first : first + count].reshape(count * cols, channels)
        total = rows_of(first, count, hidden_be, hidden_bi) + time_bias[...]
        total += (
            jnp.dot(rows_of(first, count, normed_be, normed_bi), time_kernel[0], preferred_element_type=F32)
            + jnp.dot(rows_of(first, count, normed_ae, normed_ai), time_kernel[1], preferred_element_type=F32)
            + jnp.dot(prior, time_kernel[2], preferred_element_type=F32)
        )
        decoded[first : first + count] = total.astype(BF16).reshape(count, cols, channels)

    def base_rows(first, count):
        prior = normed_p[first : first + count].reshape(count * cols, channels)
        total = rows_of(first, count, hidden_ae, hidden_ai) + time_bias[...]
        total += (
            jnp.dot(rows_of(first, count, normed_ae, normed_ai), time_kernel[0], preferred_element_type=F32)
            + jnp.dot(prior, time_kernel[1], preferred_element_type=F32)
        )
        return total

    halo = functools.partial(halo_row, counts, got_0, got_1, 2)
    get_row = framed(lambda: halo(True), edges, inners, lambda: halo(False))
    run(spatial_jobs(get_row, blocks(0, rows), 1, shifted, sums, 0, kernel,
                     (space_gain, space_bias, time_gain), emit))
    copies = []
    for n, (first, count) in enumerate(blocks(0, rows)):
        out_rows(first, count)
        copies.append(pltpu.make_async_copy(
            decoded.at[pl.ds(first, count)], out_ref.at[1, pl.ds(first, count)], sems.at[n]))
        copies[-1].start()
    for first, count in blocks(0, rows):
        base[first : first + count] = base_rows(first, count).reshape(count, cols, channels)
    for copy in copies:
        copy.wait()


def inner_finish_kernel(base, time_kernel, *refs):
    *arrived, _, decoded, out_ref, sems = refs
    cols, channels = base.shape[1:]
    keep = jnp.where(lax.axis_index("frame") > 0, 1.0, 0.0)
    kernel = (time_kernel[2].astype(F32) * keep).astype(BF16)
    start = 1
    for part in arrived:
        for row, count in blocks(start, start + part.shape[0]):
            normed = part[pl.ds(row - start, count)].reshape(count * cols, channels)
            total = base[row : row + count].reshape(count * cols, channels)
            total += jnp.dot(normed, kernel, preferred_element_type=F32)
            decoded[pl.ds(row - 1, count)] = total.astype(BF16).reshape(count, cols, channels)
        start += part.shape[0]
    copy = pltpu.make_async_copy(decoded, out_ref.at[0, pl.ds(1, decoded.shape[0])], sems.at[0])

    @pl.when(lax.axis_index("frame") > 0)
    def _():
        copy.start()
        copy.wait()


def finish_kernel(decoded, products, base, _, out_ref, edges, sems):
    rows, count = base.shape[0], decoded.shape[0]
    keep = jnp.where(lax.axis_index("frame") > 0, 1.0, 0.0)
    rest = lax.axis_index("frame") == 0
    inner = pltpu.make_async_copy(decoded, out_ref.at[0, pl.ds(1, count)], sems.at[2])
    pl.when(rest)(inner.start)
    copies = []
    for n, row in enumerate((0, rows - 1)):
        edges[n] = (base[row] + products[n].astype(F32) * keep).astype(BF16)
        copies.append(pltpu.make_async_copy(edges.at[pl.ds(n, 1)], out_ref.at[0, pl.ds(row, 1)], sems.at[n]))
        copies[-1].start()
    for copy in copies:
        copy.wait()
    pl.when(rest)(inner.wait)


def cost(pixels, taps, channels, arrays):
    return pl.CostEstimate(
        flops=2 * pixels * taps * channels * channels,
        bytes_accessed=2 * arrays * pixels * channels,
        transcendentals=2 * pixels * channels,
    )


def body(features, space_kernel, space_gain, space_bias, time_kernel, time_gain, time_bias):
    frames, rows, cols, channels = features.shape
    row = (cols, channels)
    count_f, count_b = lax.axis_size("frame"), lax.axis_size("band")
    counts = (count_f, count_b)
    onward = [(i, (i + 1) % count_f) for i in range(count_f)]
    ring = halo_ring(count_f, count_b)

    def shape(*lead, dtype=BF16):
        return jax.ShapeDtypeStruct(tuple(lead) + row, dtype)

    def room(*lead, dtype=BF16):
        return pltpu.VMEM(tuple(lead) + row, dtype)

    space_gain = space_gain.reshape(1, channels)
    time_gain = time_gain.reshape(1, channels)
    space_bias = space_bias.reshape(1, channels)
    time_bias = time_bias.reshape(1, channels)
    sums = pltpu.VMEM((4, STEP * cols, channels), F32)

    weights = (space_gain, space_bias, time_gain)
    count = len(blocks(0, rows))

    def call(kernel, inputs, outs, scratch, mebibytes, name, **more):
        inputs = [x if isinstance(x, tuple) else (VMEM, x) for x in inputs]
        specs, arrays = zip(*inputs)
        out_specs, out_shape = zip(*((VMEM, o) if not isinstance(o, tuple) else o for o in outs))
        arrays = [x if x.ndim < 3 or s is ANY else pltpu.with_memory_space_constraint(x, s.memory_space)
                  for s, x in zip(specs, arrays)]
        out_shape = [pltpu.VMEM(o.shape, o.dtype) if s is VMEM else o for s, o in zip(out_specs, out_shape)]
        return pl.pallas_call(
            kernel, in_specs=list(specs), out_specs=list(out_specs), out_shape=out_shape,
            scratch_shapes=scratch, name=name,
            compiler_params=pltpu.CompilerParams(vmem_limit_bytes=mebibytes * 1024 * 1024), **more,
        )(*arrays)

    def inner_rows(raw, start, n, scale, name, after):
        return call(
            functools.partial(inner_kernel, start), [(ANY, after), *raw, space_kernel, *weights],
            [shape(n, dtype=F32), shape(n)], [room(3, n + 2), sums],
            6, name, cost_estimate=cost(n * cols, 9 * scale, channels, 3),
        )

    held = 3 if rows >= 6 else 2
    (ends,) = call(
        functools.partial(ends_kernel, count_f), [(HBM, features)], [shape(held)],
        [pltpu.SemaphoreType.DMA((2,))], 1, "ends",
    )
    edge = [lax.ppermute(ends, "frame", onward)]
    edge_out, inner_out = call(
        load_kernel, [(ANY, ends), (HBM, features)], [shape(held), shape(rows - held)],
        [pltpu.SemaphoreType.DMA((3,))], 1, "load",
    )
    raw_a, space_kernel, time_kernel = call(
        load_rest_kernel, [(ANY, inner_out), (HBM, features), (HBM, space_kernel), (HBM, time_kernel)],
        [shape(rows), jax.ShapeDtypeStruct(space_kernel.shape, BF16),
         jax.ShapeDtypeStruct(time_kernel.shape, BF16)],
        [pltpu.SemaphoreType.DMA((3,))], 1, "load_rest",
    )
    inner = lax.ppermute(inner_out, "frame", onward)
    if count_f % 2 == 0:
        edge.append(lax.ppermute(edge_out, "frame", [(f, f ^ 1) for f in range(count_f)]))

    ring_rows = min(RING_ROWS, (rows - 2 - STEP) // STEP * STEP)
    parts = [rows - 2 - ring_rows] + [ring_rows] * (ring_rows > 0)
    inner_a = []
    if ring_rows:
        inner_a = inner_rows([raw_a], 1 + parts[0], ring_rows, 1, "inner_a_ring", raw_a)
    (edge[0],) = call(copy_kernel, [edge[0]], [shape(held)], [], 1, "arrived")
    edge, send_0, send_1 = call(
        functools.partial(halo_kernel, count_f), [raw_a, edge_out, *edge],
        [shape(held), shape(3), shape(3)], [], 1, "halo",
    )
    inner_a = [*inner_rows([raw_a], 1, parts[0], 8, "inner_a", send_0), *inner_a]
    normed_ai = inner_a[1::2]
    got_0 = lax.ppermute(send_0, ("frame", "band"), ring)
    got_1 = lax.ppermute(send_1, ("frame", "band"), [(t, s) for s, t in ring])
    arrived = [lax.ppermute(normed_ai[0], "frame", onward[:-1])]
    arrived += [lax.ppermute(part, "frame", onward) for part in normed_ai[1:]]
    hidden_bi, normed_bi = inner_rows([edge_out, inner_out], 1, rows - 2, 0, "inner_b", normed_ai[0])
    hidden_ae, normed_ae, hidden_be, normed_be, product_ae = call(
        functools.partial(edges_kernel, counts), [raw_a, edge_out, inner_out, got_0, got_1, space_kernel, *weights,
         time_kernel],
        [shape(2, dtype=F32), shape(2)] * 2 + [shape(2)], [room(4, 3, 3), sums],
        4, "edges", cost_estimate=cost(4 * cols, 9, channels, 3),
    )
    edge_arrived = lax.ppermute(product_ae, "frame", onward)

    decoded, base = call(
        functools.partial(main_kernel, counts),
        [edge, inner, got_0, got_1, space_kernel, *weights, time_kernel, time_bias,
         hidden_be, hidden_bi, normed_be, normed_bi, hidden_ae, normed_ae, *inner_a],
        [(ANY, jax.ShapeDtypeStruct(features.shape, BF16)), shape(rows, dtype=F32)],
        [room(3, rows + 2), sums, room(rows), room(rows), pltpu.SemaphoreType.DMA((count,))],
        9, "main", cost_estimate=cost(rows * cols, 14 * 8, channels, 10),
    )
    decoded_a, decoded = call(
        inner_finish_kernel, [base, time_kernel, *arrived, (ANY, decoded)],
        [shape(rows - 2), (ANY, jax.ShapeDtypeStruct(features.shape, BF16))], [pltpu.SemaphoreType.DMA((1,))],
        3, "inner_finish", input_output_aliases={2 + len(arrived): 1},
        cost_estimate=cost(rows * cols, 1, channels, 4),
    )
    (decoded,) = call(
        finish_kernel, [decoded_a, edge_arrived, base, (ANY, decoded)],
        [(ANY, jax.ShapeDtypeStruct(features.shape, BF16))], [room(2), pltpu.SemaphoreType.DMA((3,))],
        3, "finish", input_output_aliases={3: 0}, cost_estimate=cost(2 * cols, 1, channels, 4),
    )
    return decoded


def solution(mesh):
    return jax.shard_map(
        body,
        mesh=mesh,
        in_specs=(P(("grp", "frame"), "band", None, None), P(), P(), P(), P(), P(), P()),
        out_specs=P(("grp", "frame"), "band", None, None),
        check_vma=False,
    )
```

```python
import functools

import jax
import jax.numpy as jnp
from jax import lax
from jax.experimental import pallas as pl
from jax.experimental.pallas import tpu as pltpu
from jax.sharding import PartitionSpec as P

F32 = jnp.float32
BF16 = jnp.bfloat16
VMEM = pl.BlockSpec(memory_space=pltpu.VMEM)
ANY = pl.BlockSpec(memory_space=pl.ANY)
HBM = pl.BlockSpec(memory_space=pltpu.HBM)
STEP = 2
RING_ROWS = 6


def blocks(first, last):
    return [(r, min(STEP, last - r)) for r in range(first, last, STEP)]


def rms_silu(values, gain):
    mean_square = jnp.mean(values * values, axis=-1, keepdims=True)
    u = values * lax.rsqrt(mean_square + 1e-06) * (0.5 * gain)
    return u + u * jnp.tanh(u)


def norm_into(shifted, place, row, gain):
    row, scale = row if isinstance(row, tuple) else (row, None)
    normed = rms_silu(row.astype(F32), gain)
    normed = normed if scale is None else normed * scale
    cols = normed.shape[0]
    column = lax.broadcasted_iota(jnp.int32, normed.shape, 0)
    before = jnp.where(column == 0, 0.0, pltpu.roll(normed, 1, 0))
    after = jnp.where(column == cols - 1, 0.0, pltpu.roll(normed, cols - 1, 0))
    shifted[0, place] = before.astype(BF16)
    shifted[1, place] = normed.astype(BF16)
    shifted[2, place] = after.astype(BF16)


def conv_rows(shifted, kernel, place, count):
    cols, channels = shifted.shape[2:]
    total = None
    for i in range(3):
        for j in range(3):
            window = shifted[j, place + i : place + i + count].reshape(count * cols, channels)
            product = jnp.dot(window, kernel[i, j], preferred_element_type=F32)
            total = product if total is None else total + product
    return total


def spatial_jobs(get_row, row_blocks, offset, shifted, sums, slot0, kernel, weights, emit, after=None):
    space_gain, space_bias, time_gain = weights
    ready = set()
    jobs = []

    def norm_stage(first, count):
        for r in range(first - 1, first + count + 1):
            if r not in ready:
                ready.add(r)
                norm_into(shifted, r + offset, get_row(r), space_gain[...])

    def conv_stage(slot, first, count):
        total = conv_rows(shifted, kernel, first - 1 + offset, count)
        sums[slot, : total.shape[0]] = total

    def emit_stage(slot, first, count):
        own = jnp.concatenate([get_row(r) for r in range(first, first + count)], axis=0)
        hidden = own.astype(F32) + sums[slot, : own.shape[0]] + space_bias[...]
        emit(first, count, hidden, rms_silu(hidden, time_gain[...]))

    for n, (first, count) in enumerate(row_blocks):
        slot = (slot0 + n) % sums.shape[0]
        jobs.append([
            functools.partial(norm_stage, first, count),
            functools.partial(conv_stage, slot, first, count),
            functools.partial(emit_stage, slot, first, count),
            functools.partial(after, first, count) if after else None,
        ])
    return jobs


def run(jobs):
    for n in range(len(jobs) + 3):
        for stage in range(4):
            if 0 <= n - stage < len(jobs) and jobs[n - stage][stage] is not None:
                jobs[n - stage][stage]()


def wait_all(pairs, sems):
    copies = [pltpu.make_async_copy(a, b, sems.at[n]) for n, (a, b) in enumerate(pairs)]
    for copy in copies:
        copy.start()
    for copy in copies:
        copy.wait()


def end_pairs(feats, ends):
    rows, lower = feats.shape[1], ends.shape[0] // 2
    upper = ends.shape[0] - lower
    return [
        (feats.at[1, pl.ds(0, upper)], ends.at[pl.ds(0, upper)]),
        (feats.at[1, pl.ds(rows - lower, lower)], ends.at[pl.ds(upper, lower)]),
    ]


def ends_kernel(count, feats, ends, sems):
    first = first_of_pair(count)

    @pl.when(first)
    def _():
        ends[...] = jnp.zeros_like(ends)

    @pl.when(jnp.logical_not(first))
    def _():
        wait_all(end_pairs(feats, ends), sems)


def load_kernel(_, feats, ends, middle, sems):
    upper = ends.shape[0] - ends.shape[0] // 2
    wait_all(end_pairs(feats, ends) + [(feats.at[1, pl.ds(upper, middle.shape[0])], middle)], sems)


def load_rest_kernel(_, feats, kernel, time_kernel, raw_a, kernel_out, time_out, sems):
    wait_all([(feats.at[0], raw_a), (kernel, kernel_out), (time_kernel, time_out)], sems)


def goes_up(index, count):
    return index % 2 == 0 or count % 2 == 1


def halo_ring(frames, bands):
    paired = frames % 2 == 0
    pairs = []
    for f in range(frames):
        for b in range(bands):
            to = (f, b + 1) if goes_up(f, frames) else (f, b - 1)
            if not 0 <= to[1] < bands:
                if not paired:
                    continue
                to = (f ^ 1, b)
            pairs.append((f * bands + b, to[0] * bands + to[1]))
    return pairs


def up_first(count):
    index = lax.axis_index("frame")
    return lax.rem(index, 2) == 0 if count % 2 == 0 else index >= 0


def first_of_pair(count):
    index = lax.axis_index("frame")
    return lax.rem(index, 2) == 0 if count % 2 == 0 else index < 0


def copy_kernel(source, target):
    target[...] = source[...]


def halo_kernel(count, raw_a, edges_b, *refs):
    *arrived, edges, send_0, send_1 = refs
    rows = raw_a.shape[0]
    if len(arrived) == 1:
        edges[...] = arrived[0][...]
    else:
        first = first_of_pair(count)

        @pl.when(first)
        def _():
            edges[...] = arrived[0][...]

        @pl.when(jnp.logical_not(first))
        def _():
            edges[...] = arrived[1][...]

    last = edges.shape[0] - 1

    def fill(up_rows, down_rows):
        for n, (upper, lower) in enumerate((
            (raw_a.at[0], raw_a.at[rows - 1]), (edges_b.at[0], edges_b.at[last]), (edges.at[0], edges.at[last])
        )):
            up_rows[n] = lower[...]
            down_rows[n] = upper[...]

    up = up_first(count)
    pl.when(up)(lambda: fill(send_0, send_1))
    pl.when(jnp.logical_not(up))(lambda: fill(send_1, send_0))


def halo_row(counts, got_0, got_1, n, is_above):
    frames, bands = counts
    band = lax.axis_index("band")
    take = up_first(frames) if is_above else jnp.logical_not(up_first(frames))
    row = jnp.where(take, got_0[n].astype(F32), got_1[n].astype(F32))
    there = band > 0 if is_above else band < bands - 1
    return row, jnp.where(there, 1.0, 0.0)


def framed(upper, ends, middle, lower):
    middle = middle if isinstance(middle, list) else [middle]
    lower_ends, count = ends.shape[0] // 2, sum(part.shape[0] for part in middle)
    upper_ends = ends.shape[0] - lower_ends
    rows = ends.shape[0] + count

    def get_row(r):
        if r < 0 or r >= rows:
            return upper() if r < 0 else lower()
        if r < upper_ends or r >= rows - lower_ends:
            return ends[r if r < upper_ends else r - count]
        part, at = part_of(middle, r - upper_ends)
        return part[at]

    return get_row


def part_of(parts, row):
    for part in parts:
        if row < part.shape[0]:
            return part, row
        row -= part.shape[0]


def inner_emit(start, hidden_ref, normed_ref):
    def emit(first, count, hidden, normed):
        at = pl.ds(first - start, count)
        shape = (count,) + hidden_ref.shape[1:]
        hidden_ref[at] = hidden.astype(hidden_ref.dtype).reshape(shape)
        normed_ref[at] = normed.astype(BF16).reshape(shape)
    return emit


def edge_emit(hidden_ref, normed_ref):
    def emit(first, count, hidden, normed):
        which = 0 if first == 0 else 1
        hidden_ref[which] = hidden
        normed_ref[which] = normed.astype(BF16)
    return emit


def inner_kernel(start, _, *refs):
    *raw, kernel, space_gain, space_bias, time_gain, hidden_ref, normed_ref, shifted, sums = refs
    get_row = framed(None, *raw, None) if len(raw) == 2 else lambda r: raw[0][r]
    run(spatial_jobs(get_row, blocks(start, start + hidden_ref.shape[0]), 1 - start, shifted, sums, 0, kernel,
                     (space_gain, space_bias, time_gain), inner_emit(start, hidden_ref, normed_ref)))


def edges_kernel(counts, raw_a, edges_b, inners_b, got_0, got_1, kernel, space_gain, space_bias, time_gain,
                 time_kernel, hidden_a, normed_a, hidden_b, normed_b, product_a, shifted, sums):
    rows = raw_a.shape[0]
    weights = (space_gain, space_bias, time_gain)

    halo = functools.partial(halo_row, counts, got_0, got_1)

    def row_a(r):
        return halo(0, r < 0) if r < 0 or r >= rows else raw_a[r]

    row_b = framed(lambda: halo(1, True), edges_b, inners_b, lambda: halo(1, False))
    jobs = []
    for n, (get_row, emit) in enumerate((
        (row_a, edge_emit(hidden_a, normed_a)), (row_b, edge_emit(hidden_b, normed_b))
    )):
        for m, (r, offset) in enumerate(((0, 1), (rows - 1, 2 - rows))):
            jobs += spatial_jobs(get_row, [(r, 1)], offset, shifted.at[2 * n + m], sums, 2 * n + m,
                                 kernel, weights, emit)
    run(jobs)
    product = jnp.dot(normed_a[...].reshape(-1, normed_a.shape[-1]), time_kernel[2],
                      preferred_element_type=F32)
    product_a[...] = product.astype(BF16).reshape(product_a.shape)


def main_kernel(counts, edges, inners, got_0, got_1, kernel, space_gain, space_bias, time_gain,
                time_kernel, time_bias, hidden_be, hidden_bi, normed_be, normed_bi, hidden_ae, normed_ae, *refs):
    *inner_a, out_ref, base, shifted, sums, normed_p, decoded, sems = refs
    hidden_ai, normed_ai = inner_a[::2], inner_a[1::2]
    rows, cols, channels = base.shape
    keep = jnp.where(lax.axis_index("frame") > 0, 1.0, 0.0)

    def emit(first, count, hidden, normed):
        normed_p[first : first + count] = (normed * keep).astype(BF16).reshape(count, cols, channels)

    def rows_of(first, count, *parts):
        get_row = framed(None, *parts, None)
        return jnp.concatenate([get_row(r) for r in range(first, first + count)], axis=0)

    def out_rows(first, count):
        prior = normed_p[first : first + count].reshape(count * cols, channels)
        total = rows_of(first, count, hidden_be, hidden_bi) + time_bias[...]
        total += (
            jnp.dot(rows_of(first, count, normed_be, normed_bi), time_kernel[0], preferred_element_type=F32)
            + jnp.dot(rows_of(first, count, normed_ae, normed_ai), time_kernel[1], preferred_element_type=F32)
            + jnp.dot(prior, time_kernel[2], preferred_element_type=F32)
        )
        decoded[first : first + count] = total.astype(BF16).reshape(count, cols, channels)

    def base_rows(first, count):
        prior = normed_p[first : first + count].reshape(count * cols, channels)
        total = rows_of(first, count, hidden_ae, hidden_ai) + time_bias[...]
        total += (
            jnp.dot(rows_of(first, count, normed_ae, normed_ai), time_kernel[0], preferred_element_type=F32)
            + jnp.dot(prior, time_kernel[1], preferred_element_type=F32)
        )
        return total

    halo = functools.partial(halo_row, counts, got_0, got_1, 2)
    get_row = framed(lambda: halo(True), edges, inners, lambda: halo(False))
    run(spatial_jobs(get_row, blocks(0, rows), 1, shifted, sums, 0, kernel,
                     (space_gain, space_bias, time_gain), emit))
    copies = []
    for n, (first, count) in enumerate(blocks(0, rows)):
        out_rows(first, count)
        copies.append(pltpu.make_async_copy(
            decoded.at[pl.ds(first, count)], out_ref.at[1, pl.ds(first, count)], sems.at[n]))
        copies[-1].start()
    for first, count in blocks(0, rows):
        base[first : first + count] = base_rows(first, count).reshape(count, cols, channels)
    for copy in copies:
        copy.wait()


def inner_finish_kernel(base, time_kernel, *refs):
    *arrived, _, decoded, out_ref, sems = refs
    cols, channels = base.shape[1:]
    keep = jnp.where(lax.axis_index("frame") > 0, 1.0, 0.0)
    kernel = (time_kernel[2].astype(F32) * keep).astype(BF16)
    start = 1
    for part in arrived:
        for row, count in blocks(start, start + part.shape[0]):
            normed = part[pl.ds(row - start, count)].reshape(count * cols, channels)
            total = base[row : row + count].reshape(count * cols, channels)
            total += jnp.dot(normed, kernel, preferred_element_type=F32)
            decoded[pl.ds(row - 1, count)] = total.astype(BF16).reshape(count, cols, channels)
        start += part.shape[0]
    copy = pltpu.make_async_copy(decoded, out_ref.at[0, pl.ds(1, decoded.shape[0])], sems.at[0])

    @pl.when(lax.axis_index("frame") > 0)
    def _():
        copy.start()
        copy.wait()


def finish_kernel(decoded, products, base, _, out_ref, edges, sems):
    rows, count = base.shape[0], decoded.shape[0]
    keep = jnp.where(lax.axis_index("frame") > 0, 1.0, 0.0)
    rest = lax.axis_index("frame") == 0
    inner = pltpu.make_async_copy(decoded, out_ref.at[0, pl.ds(1, count)], sems.at[2])
    pl.when(rest)(inner.start)
    copies = []
    for n, row in enumerate((0, rows - 1)):
        edges[n] = (base[row] + products[n].astype(F32) * keep).astype(BF16)
        copies.append(pltpu.make_async_copy(edges.at[pl.ds(n, 1)], out_ref.at[0, pl.ds(row, 1)], sems.at[n]))
        copies[-1].start()
    for copy in copies:
        copy.wait()
    pl.when(rest)(inner.wait)


def cost(pixels, taps, channels, arrays):
    return pl.CostEstimate(
        flops=2 * pixels * taps * channels * channels,
        bytes_accessed=2 * arrays * pixels * channels,
        transcendentals=2 * pixels * channels,
    )


def body(features, space_kernel, space_gain, space_bias, time_kernel, time_gain, time_bias):
    frames, rows, cols, channels = features.shape
    row = (cols, channels)
    count_f, count_b = lax.axis_size("frame"), lax.axis_size("band")
    counts = (count_f, count_b)
    onward = [(i, (i + 1) % count_f) for i in range(count_f)]
    ring = halo_ring(count_f, count_b)

    def shape(*lead, dtype=BF16):
        return jax.ShapeDtypeStruct(tuple(lead) + row, dtype)

    def room(*lead, dtype=BF16):
        return pltpu.VMEM(tuple(lead) + row, dtype)

    space_gain = space_gain.reshape(1, channels)
    time_gain = time_gain.reshape(1, channels)
    space_bias = space_bias.reshape(1, channels)
    time_bias = time_bias.reshape(1, channels)
    sums = pltpu.VMEM((4, STEP * cols, channels), F32)

    weights = (space_gain, space_bias, time_gain)
    count = len(blocks(0, rows))

    def call(kernel, inputs, outs, scratch, mebibytes, name, **more):
        inputs = [x if isinstance(x, tuple) else (VMEM, x) for x in inputs]
        specs, arrays = zip(*inputs)
        out_specs, out_shape = zip(*((VMEM, o) if not isinstance(o, tuple) else o for o in outs))
        arrays = [x if x.ndim < 3 or s is ANY else pltpu.with_memory_space_constraint(x, s.memory_space)
                  for s, x in zip(specs, arrays)]
        out_shape = [pltpu.VMEM(o.shape, o.dtype) if s is VMEM else o for s, o in zip(out_specs, out_shape)]
        return pl.pallas_call(
            kernel, in_specs=list(specs), out_specs=list(out_specs), out_shape=out_shape,
            scratch_shapes=scratch, name=name,
            compiler_params=pltpu.CompilerParams(vmem_limit_bytes=mebibytes * 1024 * 1024), **more,
        )(*arrays)

    def inner_rows(raw, start, n, scale, name, after):
        return call(
            functools.partial(inner_kernel, start), [(ANY, after), *raw, space_kernel, *weights],
            [shape(n, dtype=F32), shape(n)], [room(3, n + 2), sums],
            6, name, cost_estimate=cost(n * cols, 9 * scale, channels, 3),
        )

    held = 3 if rows >= 6 else 2
    (ends,) = call(
        functools.partial(ends_kernel, count_f), [(HBM, features)], [shape(held)],
        [pltpu.SemaphoreType.DMA((2,))], 1, "ends",
    )
    edge = [lax.ppermute(ends, "frame", onward)]
    edge_out, inner_out = call(
        load_kernel, [(ANY, ends), (HBM, features)], [shape(held), shape(rows - held)],
        [pltpu.SemaphoreType.DMA((3,))], 1, "load",
    )
    raw_a, space_kernel, time_kernel = call(
        load_rest_kernel, [(ANY, inner_out), (HBM, features), (HBM, space_kernel), (HBM, time_kernel)],
        [shape(rows), jax.ShapeDtypeStruct(space_kernel.shape, BF16),
         jax.ShapeDtypeStruct(time_kernel.shape, BF16)],
        [pltpu.SemaphoreType.DMA((3,))], 1, "load_rest",
    )
    inner = lax.ppermute(inner_out, "frame", onward)
    if count_f % 2 == 0:
        edge.append(lax.ppermute(edge_out, "frame", [(f, f ^ 1) for f in range(count_f)]))

    ring_rows = min(RING_ROWS, (rows - 2 - STEP) // STEP * STEP)
    parts = [rows - 2 - ring_rows] + [ring_rows] * (ring_rows > 0)
    inner_a = []
    if ring_rows:
        inner_a = inner_rows([raw_a], 1 + parts[0], ring_rows, 1, "inner_a_ring", raw_a)
    (edge[0],) = call(copy_kernel, [edge[0]], [shape(held)], [], 1, "arrived")
    edge, send_0, send_1 = call(
        functools.partial(halo_kernel, count_f), [raw_a, edge_out, *edge],
        [shape(held), shape(3), shape(3)], [], 1, "halo",
    )
    inner_a = [*inner_rows([raw_a], 1, parts[0], 8, "inner_a", send_0), *inner_a]
    normed_ai = inner_a[1::2]
    got_0 = lax.ppermute(send_0, ("frame", "band"), ring)
    got_1 = lax.ppermute(send_1, ("frame", "band"), [(t, s) for s, t in ring])
    arrived = [lax.ppermute(normed_ai[0], "frame", onward[:-1])]
    arrived += [lax.ppermute(part, "frame", onward) for part in normed_ai[1:]]
    hidden_bi, normed_bi = inner_rows([edge_out, inner_out], 1, rows - 2, 1, "inner_b", normed_ai[0])
    hidden_ae, normed_ae, hidden_be, normed_be, product_ae = call(
        functools.partial(edges_kernel, counts), [raw_a, edge_out, inner_out, got_0, got_1, space_kernel, *weights,
         time_kernel],
        [shape(2, dtype=F32), shape(2)] * 2 + [shape(2)], [room(4, 3, 3), sums],
        4, "edges", cost_estimate=cost(4 * cols, 9, channels, 3),
    )
    edge_arrived = lax.ppermute(product_ae, "frame", onward)

    decoded, base = call(
        functools.partial(main_kernel, counts),
        [edge, inner, got_0, got_1, space_kernel, *weights, time_kernel, time_bias,
         hidden_be, hidden_bi, normed_be, normed_bi, hidden_ae, normed_ae, *inner_a],
        [(ANY, jax.ShapeDtypeStruct(features.shape, BF16)), shape(rows, dtype=F32)],
        [room(3, rows + 2), sums, room(rows), room(rows), pltpu.SemaphoreType.DMA((count,))],
        9, "main", cost_estimate=cost(rows * cols, 14 * 8, channels, 10),
    )
    decoded_a, decoded = call(
        inner_finish_kernel, [base, time_kernel, *arrived, (ANY, decoded)],
        [shape(rows - 2), (ANY, jax.ShapeDtypeStruct(features.shape, BF16))], [pltpu.SemaphoreType.DMA((1,))],
        3, "inner_finish", input_output_aliases={2 + len(arrived): 1},
        cost_estimate=cost(rows * cols, 1, channels, 4),
    )
    (decoded,) = call(
        finish_kernel, [decoded_a, edge_arrived, base, (ANY, decoded)],
        [(ANY, jax.ShapeDtypeStruct(features.shape, BF16))], [room(2), pltpu.SemaphoreType.DMA((3,))],
        3, "finish", input_output_aliases={3: 0}, cost_estimate=cost(2 * cols, 1, channels, 4),
    )
    return decoded


def solution(mesh):
    return jax.shard_map(
        body,
        mesh=mesh,
        in_specs=(P(("grp", "frame"), "band", None, None), P(), P(), P(), P(), P(), P()),
        out_specs=P(("grp", "frame"), "band", None, None),
        check_vma=False,
    )
```

```python
import functools

import jax
import jax.numpy as jnp
from jax import lax
from jax.experimental import pallas as pl
from jax.experimental.pallas import tpu as pltpu
from jax.sharding import PartitionSpec as P

F32 = jnp.float32
BF16 = jnp.bfloat16
VMEM = pl.BlockSpec(memory_space=pltpu.VMEM)
ANY = pl.BlockSpec(memory_space=pl.ANY)
HBM = pl.BlockSpec(memory_space=pltpu.HBM)
STEP = 2
RING_ROWS = 6


def blocks(first, last):
    return [(r, min(STEP, last - r)) for r in range(first, last, STEP)]


def rms_silu(values, gain):
    mean_square = jnp.mean(values * values, axis=-1, keepdims=True)
    u = values * lax.rsqrt(mean_square + 1e-06) * (0.5 * gain)
    return u + u * jnp.tanh(u)


def norm_into(shifted, place, row, gain):
    row, scale = row if isinstance(row, tuple) else (row, None)
    normed = rms_silu(row.astype(F32), gain)
    normed = normed if scale is None else normed * scale
    cols = normed.shape[0]
    column = lax.broadcasted_iota(jnp.int32, normed.shape, 0)
    before = jnp.where(column == 0, 0.0, pltpu.roll(normed, 1, 0))
    after = jnp.where(column == cols - 1, 0.0, pltpu.roll(normed, cols - 1, 0))
    shifted[0, place] = before.astype(BF16)
    shifted[1, place] = normed.astype(BF16)
    shifted[2, place] = after.astype(BF16)


def conv_rows(shifted, kernel, place, count):
    cols, channels = shifted.shape[2:]
    total = None
    for i in range(3):
        for j in range(3):
            window = shifted[j, place + i : place + i + count].reshape(count * cols, channels)
            product = jnp.dot(window, kernel[i, j], preferred_element_type=F32)
            total = product if total is None else total + product
    return total


def spatial_jobs(get_row, row_blocks, offset, shifted, sums, slot0, kernel, weights, emit, after=None):
    space_gain, space_bias, time_gain = weights
    ready = set()
    jobs = []

    def norm_stage(first, count):
        for r in range(first - 1, first + count + 1):
            if r not in ready:
                ready.add(r)
                norm_into(shifted, r + offset, get_row(r), space_gain[...])

    def conv_stage(slot, first, count):
        total = conv_rows(shifted, kernel, first - 1 + offset, count)
        sums[slot, : total.shape[0]] = total

    def emit_stage(slot, first, count):
        own = jnp.concatenate([get_row(r) for r in range(first, first + count)], axis=0)
        hidden = own.astype(F32) + sums[slot, : own.shape[0]] + space_bias[...]
        emit(first, count, hidden, rms_silu(hidden, time_gain[...]))

    for n, (first, count) in enumerate(row_blocks):
        slot = (slot0 + n) % sums.shape[0]
        jobs.append([
            functools.partial(norm_stage, first, count),
            functools.partial(conv_stage, slot, first, count),
            functools.partial(emit_stage, slot, first, count),
            functools.partial(after, first, count) if after else None,
        ])
    return jobs


def run(jobs):
    for n in range(len(jobs) + 3):
        for stage in range(4):
            if 0 <= n - stage < len(jobs) and jobs[n - stage][stage] is not None:
                jobs[n - stage][stage]()


def wait_all(pairs, sems):
    copies = [pltpu.make_async_copy(a, b, sems.at[n]) for n, (a, b) in enumerate(pairs)]
    for copy in copies:
        copy.start()
    for copy in copies:
        copy.wait()


def end_pairs(feats, ends):
    rows, lower = feats.shape[1], ends.shape[0] // 2
    upper = ends.shape[0] - lower
    return [
        (feats.at[1, pl.ds(0, upper)], ends.at[pl.ds(0, upper)]),
        (feats.at[1, pl.ds(rows - lower, lower)], ends.at[pl.ds(upper, lower)]),
    ]


def ends_kernel(count, feats, ends, sems):
    first = first_of_pair(count)

    @pl.when(first)
    def _():
        ends[...] = jnp.zeros_like(ends)

    @pl.when(jnp.logical_not(first))
    def _():
        wait_all(end_pairs(feats, ends), sems)


def load_kernel(_, feats, ends, middle, sems):
    upper = ends.shape[0] - ends.shape[0] // 2
    wait_all(end_pairs(feats, ends) + [(feats.at[1, pl.ds(upper, middle.shape[0])], middle)], sems)


def load_rest_kernel(_, feats, kernel, time_kernel, raw_a, kernel_out, time_out, sems):
    wait_all([(feats.at[0], raw_a), (kernel, kernel_out), (time_kernel, time_out)], sems)


def goes_up(index, count):
    return index % 2 == 0 or count % 2 == 1


def halo_ring(frames, bands):
    paired = frames % 2 == 0
    pairs = []
    for f in range(frames):
        for b in range(bands):
            to = (f, b + 1) if goes_up(f, frames) else (f, b - 1)
            if not 0 <= to[1] < bands:
                if not paired:
                    continue
                to = (f ^ 1, b)
            pairs.append((f * bands + b, to[0] * bands + to[1]))
    return pairs


def up_first(count):
    index = lax.axis_index("frame")
    return lax.rem(index, 2) == 0 if count % 2 == 0 else index >= 0


def first_of_pair(count):
    index = lax.axis_index("frame")
    return lax.rem(index, 2) == 0 if count % 2 == 0 else index < 0


def copy_kernel(source, target):
    target[...] = source[...]


def halo_kernel(count, raw_a, edges_b, *refs):
    *arrived, edges, send_0, send_1 = refs
    rows = raw_a.shape[0]
    if len(arrived) == 1:
        edges[...] = arrived[0][...]
    else:
        first = first_of_pair(count)

        @pl.when(first)
        def _():
            edges[...] = arrived[0][...]

        @pl.when(jnp.logical_not(first))
        def _():
            edges[...] = arrived[1][...]

    last = edges.shape[0] - 1

    def fill(up_rows, down_rows):
        for n, (upper, lower) in enumerate((
            (raw_a.at[0], raw_a.at[rows - 1]), (edges_b.at[0], edges_b.at[last]), (edges.at[0], edges.at[last])
        )):
            up_rows[n] = lower[...]
            down_rows[n] = upper[...]

    up = up_first(count)
    pl.when(up)(lambda: fill(send_0, send_1))
    pl.when(jnp.logical_not(up))(lambda: fill(send_1, send_0))


def halo_row(counts, got_0, got_1, n, is_above):
    frames, bands = counts
    band = lax.axis_index("band")
    take = up_first(frames) if is_above else jnp.logical_not(up_first(frames))
    row = jnp.where(take, got_0[n].astype(F32), got_1[n].astype(F32))
    there = band > 0 if is_above else band < bands - 1
    return row, jnp.where(there, 1.0, 0.0)


def framed(upper, ends, middle, lower):
    middle = middle if isinstance(middle, list) else [middle]
    lower_ends, count = ends.shape[0] // 2, sum(part.shape[0] for part in middle)
    upper_ends = ends.shape[0] - lower_ends
    rows = ends.shape[0] + count

    def get_row(r):
        if r < 0 or r >= rows:
            return upper() if r < 0 else lower()
        if r < upper_ends or r >= rows - lower_ends:
            return ends[r if r < upper_ends else r - count]
        part, at = part_of(middle, r - upper_ends)
        return part[at]

    return get_row


def part_of(parts, row):
    for part in parts:
        if row < part.shape[0]:
            return part, row
        row -= part.shape[0]


def inner_emit(start, hidden_ref, normed_ref):
    def emit(first, count, hidden, normed):
        at = pl.ds(first - start, count)
        shape = (count,) + hidden_ref.shape[1:]
        hidden_ref[at] = hidden.astype(hidden_ref.dtype).reshape(shape)
        normed_ref[at] = normed.astype(BF16).reshape(shape)
    return emit


def edge_emit(hidden_ref, normed_ref):
    def emit(first, count, hidden, normed):
        which = 0 if first == 0 else 1
        hidden_ref[which] = hidden
        normed_ref[which] = normed.astype(BF16)
    return emit


def inner_kernel(start, _, *refs):
    *raw, kernel, space_gain, space_bias, time_gain, hidden_ref, normed_ref, shifted, sums = refs
    get_row = framed(None, *raw, None) if len(raw) == 2 else lambda r: raw[0][r]
    run(spatial_jobs(get_row, blocks(start, start + hidden_ref.shape[0]), 1 - start, shifted, sums, 0, kernel,
                     (space_gain, space_bias, time_gain), inner_emit(start, hidden_ref, normed_ref)))


def edges_kernel(counts, raw_a, edges_b, inners_b, got_0, got_1, kernel, space_gain, space_bias, time_gain,
                 time_kernel, hidden_a, normed_a, hidden_b, normed_b, product_a, shifted, sums):
    rows = raw_a.shape[0]
    weights = (space_gain, space_bias, time_gain)

    halo = functools.partial(halo_row, counts, got_0, got_1)

    def row_a(r):
        return halo(0, r < 0) if r < 0 or r >= rows else raw_a[r]

    row_b = framed(lambda: halo(1, True), edges_b, inners_b, lambda: halo(1, False))
    jobs = []
    for n, (get_row, emit) in enumerate((
        (row_a, edge_emit(hidden_a, normed_a)), (row_b, edge_emit(hidden_b, normed_b))
    )):
        for m, (r, offset) in enumerate(((0, 1), (rows - 1, 2 - rows))):
            jobs += spatial_jobs(get_row, [(r, 1)], offset, shifted.at[2 * n + m], sums, 2 * n + m,
                                 kernel, weights, emit)
    run(jobs)
    product = jnp.dot(normed_a[...].reshape(-1, normed_a.shape[-1]), time_kernel[2],
                      preferred_element_type=F32)
    product_a[...] = product.astype(BF16).reshape(product_a.shape)


def main_kernel(counts, edges, inners, got_0, got_1, kernel, space_gain, space_bias, time_gain,
                time_kernel, time_bias, hidden_be, hidden_bi, normed_be, normed_bi, hidden_ae, normed_ae, *refs):
    *inner_a, out_ref, base, shifted, sums, normed_p, decoded, sems = refs
    hidden_ai, normed_ai = inner_a[::2], inner_a[1::2]
    rows, cols, channels = base.shape
    keep = jnp.where(lax.axis_index("frame") > 0, 1.0, 0.0)

    def emit(first, count, hidden, normed):
        normed_p[first : first + count] = (normed * keep).astype(BF16).reshape(count, cols, channels)

    def rows_of(first, count, *parts):
        get_row = framed(None, *parts, None)
        return jnp.concatenate([get_row(r) for r in range(first, first + count)], axis=0)

    def out_rows(first, count):
        prior = normed_p[first : first + count].reshape(count * cols, channels)
        total = rows_of(first, count, hidden_be, hidden_bi) + time_bias[...]
        total += (
            jnp.dot(rows_of(first, count, normed_be, normed_bi), time_kernel[0], preferred_element_type=F32)
            + jnp.dot(rows_of(first, count, normed_ae, normed_ai), time_kernel[1], preferred_element_type=F32)
            + jnp.dot(prior, time_kernel[2], preferred_element_type=F32)
        )
        decoded[first : first + count] = total.astype(BF16).reshape(count, cols, channels)

    def base_rows(first, count):
        prior = normed_p[first : first + count].reshape(count * cols, channels)
        total = rows_of(first, count, hidden_ae, hidden_ai) + time_bias[...]
        total += (
            jnp.dot(rows_of(first, count, normed_ae, normed_ai), time_kernel[0], preferred_element_type=F32)
            + jnp.dot(prior, time_kernel[1], preferred_element_type=F32)
        )
        return total

    halo = functools.partial(halo_row, counts, got_0, got_1, 2)
    get_row = framed(lambda: halo(True), edges, inners, lambda: halo(False))
    run(spatial_jobs(get_row, blocks(0, rows), 1, shifted, sums, 0, kernel,
                     (space_gain, space_bias, time_gain), emit))
    copies = []
    for n, (first, count) in enumerate(blocks(0, rows)):
        out_rows(first, count)
        copies.append(pltpu.make_async_copy(
            decoded.at[pl.ds(first, count)], out_ref.at[1, pl.ds(first, count)], sems.at[n]))
        copies[-1].start()
    for first, count in blocks(0, rows):
        base[first : first + count] = base_rows(first, count).reshape(count, cols, channels)
    for copy in copies:
        copy.wait()


def ends_late(count):
    index = lax.axis_index("frame")
    return jnp.logical_and(lax.rem(index, 2) == 0, index > 0) if count % 2 == 0 else index >= 0


def write_edges(products, base, out_ref, edges, sems):
    rows = base.shape[0]
    keep = jnp.where(lax.axis_index("frame") > 0, 1.0, 0.0)
    copies = []
    for n, row in enumerate((0, rows - 1)):
        edges[n] = (base[row] + products[n].astype(F32) * keep).astype(BF16)
        copies.append(pltpu.make_async_copy(edges.at[pl.ds(n, 1)], out_ref.at[0, pl.ds(row, 1)], sems.at[n]))
        copies[-1].start()
    for copy in copies:
        copy.wait()


def inner_finish_kernel(frames, base, time_kernel, products, *refs):
    *arrived, _, out_ref, decoded, edges, sems = refs
    cols, channels = base.shape[1:]
    keep = jnp.where(lax.axis_index("frame") > 0, 1.0, 0.0)
    kernel = (time_kernel[2].astype(F32) * keep).astype(BF16)
    start = 1
    for part in arrived:
        for row, count in blocks(start, start + part.shape[0]):
            normed = part[pl.ds(row - start, count)].reshape(count * cols, channels)
            total = base[row : row + count].reshape(count * cols, channels)
            total += jnp.dot(normed, kernel, preferred_element_type=F32)
            decoded[pl.ds(row - 1, count)] = total.astype(BF16).reshape(count, cols, channels)
        start += part.shape[0]
    copy = pltpu.make_async_copy(decoded, out_ref.at[0, pl.ds(1, decoded.shape[0])], sems.at[2])
    copy.start()
    pl.when(jnp.logical_not(ends_late(frames)))(lambda: write_edges(products, base, out_ref, edges, sems))
    copy.wait()


def finish_kernel(frames, products, base, _, out_ref, edges, sems):
    pl.when(ends_late(frames))(lambda: write_edges(products, base, out_ref, edges, sems))


def cost(pixels, taps, channels, arrays):
    return pl.CostEstimate(
        flops=2 * pixels * taps * channels * channels,
        bytes_accessed=2 * arrays * pixels * channels,
        transcendentals=2 * pixels * channels,
    )


def body(features, space_kernel, space_gain, space_bias, time_kernel, time_gain, time_bias):
    frames, rows, cols, channels = features.shape
    row = (cols, channels)
    count_f, count_b = lax.axis_size("frame"), lax.axis_size("band")
    counts = (count_f, count_b)
    onward = [(i, (i + 1) % count_f) for i in range(count_f)]
    ring = halo_ring(count_f, count_b)

    def shape(*lead, dtype=BF16):
        return jax.ShapeDtypeStruct(tuple(lead) + row, dtype)

    def room(*lead, dtype=BF16):
        return pltpu.VMEM(tuple(lead) + row, dtype)

    space_gain = space_gain.reshape(1, channels)
    time_gain = time_gain.reshape(1, channels)
    space_bias = space_bias.reshape(1, channels)
    time_bias = time_bias.reshape(1, channels)
    sums = pltpu.VMEM((4, STEP * cols, channels), F32)

    weights = (space_gain, space_bias, time_gain)
    count = len(blocks(0, rows))

    def call(kernel, inputs, outs, scratch, mebibytes, name, **more):
        inputs = [x if isinstance(x, tuple) else (VMEM, x) for x in inputs]
        specs, arrays = zip(*inputs)
        out_specs, out_shape = zip(*((VMEM, o) if not isinstance(o, tuple) else o for o in outs))
        arrays = [x if x.ndim < 3 or s is ANY else pltpu.with_memory_space_constraint(x, s.memory_space)
                  for s, x in zip(specs, arrays)]
        out_shape = [pltpu.VMEM(o.shape, o.dtype) if s is VMEM else o for s, o in zip(out_specs, out_shape)]
        return pl.pallas_call(
            kernel, in_specs=list(specs), out_specs=list(out_specs), out_shape=out_shape,
            scratch_shapes=scratch, name=name,
            compiler_params=pltpu.CompilerParams(vmem_limit_bytes=mebibytes * 1024 * 1024), **more,
        )(*arrays)

    def inner_rows(raw, start, n, scale, name, after):
        return call(
            functools.partial(inner_kernel, start), [(ANY, after), *raw, space_kernel, *weights],
            [shape(n, dtype=F32), shape(n)], [room(3, n + 2), sums],
            6, name, cost_estimate=cost(n * cols, 9 * scale, channels, 3),
        )

    held = 3 if rows >= 6 else 2
    (ends,) = call(
        functools.partial(ends_kernel, count_f), [(HBM, features)], [shape(held)],
        [pltpu.SemaphoreType.DMA((2,))], 1, "ends",
    )
    edge = [lax.ppermute(ends, "frame", onward)]
    edge_out, inner_out = call(
        load_kernel, [(ANY, ends), (HBM, features)], [shape(held), shape(rows - held)],
        [pltpu.SemaphoreType.DMA((3,))], 1, "load",
    )
    raw_a, space_kernel, time_kernel = call(
        load_rest_kernel, [(ANY, inner_out), (HBM, features), (HBM, space_kernel), (HBM, time_kernel)],
        [shape(rows), jax.ShapeDtypeStruct(space_kernel.shape, BF16),
         jax.ShapeDtypeStruct(time_kernel.shape, BF16)],
        [pltpu.SemaphoreType.DMA((3,))], 1, "load_rest",
    )
    inner = lax.ppermute(inner_out, "frame", onward)
    if count_f % 2 == 0:
        edge.append(lax.ppermute(edge_out, "frame", [(f, f ^ 1) for f in range(count_f)]))

    ring_rows = min(RING_ROWS, (rows - 2 - STEP) // STEP * STEP)
    parts = [rows - 2 - ring_rows] + [ring_rows] * (ring_rows > 0)
    inner_a = []
    if ring_rows:
        inner_a = inner_rows([raw_a], 1 + parts[0], ring_rows, 1, "inner_a_ring", raw_a)
    (edge[0],) = call(copy_kernel, [edge[0]], [shape(held)], [], 1, "arrived")
    edge, send_0, send_1 = call(
        functools.partial(halo_kernel, count_f), [raw_a, edge_out, *edge],
        [shape(held), shape(3), shape(3)], [], 1, "halo",
    )
    inner_a = [*inner_rows([raw_a], 1, parts[0], 8, "inner_a", send_0), *inner_a]
    normed_ai = inner_a[1::2]
    got_0 = lax.ppermute(send_0, ("frame", "band"), ring)
    got_1 = lax.ppermute(send_1, ("frame", "band"), [(t, s) for s, t in ring])
    arrived = [lax.ppermute(normed_ai[0], "frame", onward[:-1])]
    arrived += [lax.ppermute(part, "frame", onward) for part in normed_ai[1:]]
    hidden_bi, normed_bi = inner_rows([edge_out, inner_out], 1, rows - 2, 1, "inner_b", normed_ai[0])
    hidden_ae, normed_ae, hidden_be, normed_be, product_ae = call(
        functools.partial(edges_kernel, counts), [raw_a, edge_out, inner_out, got_0, got_1, space_kernel, *weights,
         time_kernel],
        [shape(2, dtype=F32), shape(2)] * 2 + [shape(2)], [room(4, 3, 3), sums],
        4, "edges", cost_estimate=cost(4 * cols, 9, channels, 3),
    )
    edge_arrived = lax.ppermute(product_ae, "frame", onward)
    edge_swapped = edge_arrived
    if count_f % 2 == 0:
        edge_swapped = lax.ppermute(product_ae, "frame", [(f, f ^ 1) for f in range(count_f)])

    decoded, base = call(
        functools.partial(main_kernel, counts),
        [edge, inner, got_0, got_1, space_kernel, *weights, time_kernel, time_bias,
         hidden_be, hidden_bi, normed_be, normed_bi, hidden_ae, normed_ae, *inner_a],
        [(ANY, jax.ShapeDtypeStruct(features.shape, BF16)), shape(rows, dtype=F32)],
        [room(3, rows + 2), sums, room(rows), room(rows), pltpu.SemaphoreType.DMA((count,))],
        9, "main", cost_estimate=cost(rows * cols, 14 * 8, channels, 10),
    )
    out = (ANY, jax.ShapeDtypeStruct(features.shape, BF16))
    (decoded,) = call(
        functools.partial(inner_finish_kernel, count_f),
        [base, time_kernel, edge_swapped, *arrived, (ANY, decoded)], [out],
        [room(rows - 2), room(2), pltpu.SemaphoreType.DMA((3,))],
        3, "inner_finish", input_output_aliases={3 + len(arrived): 0},
        cost_estimate=cost(rows * cols, 1, channels, 4),
    )
    (decoded,) = call(
        functools.partial(finish_kernel, count_f), [edge_arrived, base, (ANY, decoded)], [out],
        [room(2), pltpu.SemaphoreType.DMA((2,))],
        3, "finish", input_output_aliases={2: 0}, cost_estimate=cost(2 * cols, 1, channels, 4),
    )
    return decoded


def solution(mesh):
    return jax.shard_map(
        body,
        mesh=mesh,
        in_specs=(P(("grp", "frame"), "band", None, None), P(), P(), P(), P(), P(), P()),
        out_specs=P(("grp", "frame"), "band", None, None),
        check_vma=False,
    )
```

```python
import functools

import jax
import jax.numpy as jnp
from jax import lax
from jax.experimental import pallas as pl
from jax.experimental.pallas import tpu as pltpu
from jax.sharding import PartitionSpec as P

F32 = jnp.float32
BF16 = jnp.bfloat16
VMEM = pl.BlockSpec(memory_space=pltpu.VMEM)
ANY = pl.BlockSpec(memory_space=pl.ANY)
HBM = pl.BlockSpec(memory_space=pltpu.HBM)
STEP = 2
RING_ROWS = 6


def blocks(first, last):
    return [(r, min(STEP, last - r)) for r in range(first, last, STEP)]


def rms_silu(values, gain):
    mean_square = jnp.mean(values * values, axis=-1, keepdims=True)
    u = values * lax.rsqrt(mean_square + 1e-06) * (0.5 * gain)
    return u + u * jnp.tanh(u)


def norm_into(shifted, place, row, gain):
    row, scale = row if isinstance(row, tuple) else (row, None)
    normed = rms_silu(row.astype(F32), gain)
    normed = normed if scale is None else normed * scale
    cols = normed.shape[0]
    column = lax.broadcasted_iota(jnp.int32, normed.shape, 0)
    before = jnp.where(column == 0, 0.0, pltpu.roll(normed, 1, 0))
    after = jnp.where(column == cols - 1, 0.0, pltpu.roll(normed, cols - 1, 0))
    shifted[0, place] = before.astype(BF16)
    shifted[1, place] = normed.astype(BF16)
    shifted[2, place] = after.astype(BF16)


def conv_rows(shifted, kernel, place, count):
    cols, channels = shifted.shape[2:]
    total = None
    for i in range(3):
        for j in range(3):
            window = shifted[j, place + i : place + i + count].reshape(count * cols, channels)
            product = jnp.dot(window, kernel[i, j], preferred_element_type=F32)
            total = product if total is None else total + product
    return total


def spatial_jobs(get_row, row_blocks, offset, shifted, sums, slot0, kernel, weights, emit, after=None):
    space_gain, space_bias, time_gain = weights
    ready = set()
    jobs = []

    def norm_stage(first, count):
        for r in range(first - 1, first + count + 1):
            if r not in ready:
                ready.add(r)
                norm_into(shifted, r + offset, get_row(r), space_gain[...])

    def conv_stage(slot, first, count):
        total = conv_rows(shifted, kernel, first - 1 + offset, count)
        sums[slot, : total.shape[0]] = total

    def emit_stage(slot, first, count):
        own = jnp.concatenate([get_row(r) for r in range(first, first + count)], axis=0)
        hidden = own.astype(F32) + sums[slot, : own.shape[0]] + space_bias[...]
        emit(first, count, hidden, rms_silu(hidden, time_gain[...]))

    for n, (first, count) in enumerate(row_blocks):
        slot = (slot0 + n) % sums.shape[0]
        jobs.append([
            functools.partial(norm_stage, first, count),
            functools.partial(conv_stage, slot, first, count),
            functools.partial(emit_stage, slot, first, count),
            functools.partial(after, first, count) if after else None,
        ])
    return jobs


def run(jobs):
    for n in range(len(jobs) + 3):
        for stage in range(4):
            if 0 <= n - stage < len(jobs) and jobs[n - stage][stage] is not None:
                jobs[n - stage][stage]()


def wait_all(pairs, sems):
    copies = [pltpu.make_async_copy(a, b, sems.at[n]) for n, (a, b) in enumerate(pairs)]
    for copy in copies:
        copy.start()
    for copy in copies:
        copy.wait()


def end_pairs(feats, ends):
    rows, lower = feats.shape[1], ends.shape[0] // 2
    upper = ends.shape[0] - lower
    return [
        (feats.at[1, pl.ds(0, upper)], ends.at[pl.ds(0, upper)]),
        (feats.at[1, pl.ds(rows - lower, lower)], ends.at[pl.ds(upper, lower)]),
    ]


def ends_kernel(count, feats, ends, sems):
    first = first_of_pair(count)

    @pl.when(first)
    def _():
        ends[...] = jnp.zeros_like(ends)

    @pl.when(jnp.logical_not(first))
    def _():
        wait_all(end_pairs(feats, ends), sems)


def load_kernel(_, feats, ends, middle, sems):
    upper = ends.shape[0] - ends.shape[0] // 2
    wait_all(end_pairs(feats, ends) + [(feats.at[1, pl.ds(upper, middle.shape[0])], middle)], sems)


def load_rest_kernel(_, feats, kernel, time_kernel, raw_a, kernel_out, time_out, sems):
    wait_all([(feats.at[0], raw_a), (kernel, kernel_out), (time_kernel, time_out)], sems)


def goes_up(index, count):
    return index % 2 == 0 or count % 2 == 1


def halo_ring(frames, bands):
    paired = frames % 2 == 0
    pairs = []
    for f in range(frames):
        for b in range(bands):
            to = (f, b + 1) if goes_up(f, frames) else (f, b - 1)
            if not 0 <= to[1] < bands:
                if not paired:
                    continue
                to = (f ^ 1, b)
            pairs.append((f * bands + b, to[0] * bands + to[1]))
    return pairs


def up_first(count):
    index = lax.axis_index("frame")
    return lax.rem(index, 2) == 0 if count % 2 == 0 else index >= 0


def first_of_pair(count):
    index = lax.axis_index("frame")
    return lax.rem(index, 2) == 0 if count % 2 == 0 else index < 0


def copy_kernel(source, target):
    target[...] = source[...]


def halo_kernel(count, raw_a, edges_b, *refs):
    *arrived, edges, send_0, send_1 = refs
    rows = raw_a.shape[0]
    if len(arrived) == 1:
        edges[...] = arrived[0][...]
    else:
        first = first_of_pair(count)

        @pl.when(first)
        def _():
            edges[...] = arrived[0][...]

        @pl.when(jnp.logical_not(first))
        def _():
            edges[...] = arrived[1][...]

    last = edges.shape[0] - 1

    def fill(up_rows, down_rows):
        for n, (upper, lower) in enumerate((
            (raw_a.at[0], raw_a.at[rows - 1]), (edges_b.at[0], edges_b.at[last]), (edges.at[0], edges.at[last])
        )):
            up_rows[n] = lower[...]
            down_rows[n] = upper[...]

    up = up_first(count)
    pl.when(up)(lambda: fill(send_0, send_1))
    pl.when(jnp.logical_not(up))(lambda: fill(send_1, send_0))


def halo_row(counts, got_0, got_1, n, is_above):
    frames, bands = counts
    band = lax.axis_index("band")
    take = up_first(frames) if is_above else jnp.logical_not(up_first(frames))
    row = jnp.where(take, got_0[n].astype(F32), got_1[n].astype(F32))
    there = band > 0 if is_above else band < bands - 1
    return row, jnp.where(there, 1.0, 0.0)


def framed(upper, ends, middle, lower):
    middle = middle if isinstance(middle, list) else [middle]
    lower_ends, count = ends.shape[0] // 2, sum(part.shape[0] for part in middle)
    upper_ends = ends.shape[0] - lower_ends
    rows = ends.shape[0] + count

    def get_row(r):
        if r < 0 or r >= rows:
            return upper() if r < 0 else lower()
        if r < upper_ends or r >= rows - lower_ends:
            return ends[r if r < upper_ends else r - count]
        part, at = part_of(middle, r - upper_ends)
        return part[at]

    return get_row


def part_of(parts, row):
    for part in parts:
        if row < part.shape[0]:
            return part, row
        row -= part.shape[0]


def inner_emit(start, hidden_ref, normed_ref):
    def emit(first, count, hidden, normed):
        at = pl.ds(first - start, count)
        shape = (count,) + hidden_ref.shape[1:]
        hidden_ref[at] = hidden.astype(hidden_ref.dtype).reshape(shape)
        normed_ref[at] = normed.astype(BF16).reshape(shape)
    return emit


def edge_emit(hidden_ref, normed_ref):
    def emit(first, count, hidden, normed):
        which = 0 if first == 0 else 1
        hidden_ref[which] = hidden
        normed_ref[which] = normed.astype(BF16)
    return emit


def inner_kernel(start, _, *refs):
    *raw, kernel, space_gain, space_bias, time_gain, hidden_ref, normed_ref, shifted, sums = refs
    get_row = framed(None, *raw, None) if len(raw) == 2 else lambda r: raw[0][r]
    run(spatial_jobs(get_row, blocks(start, start + hidden_ref.shape[0]), 1 - start, shifted, sums, 0, kernel,
                     (space_gain, space_bias, time_gain), inner_emit(start, hidden_ref, normed_ref)))


def edges_kernel(counts, raw_a, edges_b, inners_b, got_0, got_1, kernel, space_gain, space_bias, time_gain,
                 time_kernel, hidden_a, normed_a, hidden_b, normed_b, product_a, shifted, sums):
    rows = raw_a.shape[0]
    weights = (space_gain, space_bias, time_gain)

    halo = functools.partial(halo_row, counts, got_0, got_1)

    def row_a(r):
        return halo(0, r < 0) if r < 0 or r >= rows else raw_a[r]

    row_b = framed(lambda: halo(1, True), edges_b, inners_b, lambda: halo(1, False))
    jobs = []
    for n, (get_row, emit) in enumerate((
        (row_a, edge_emit(hidden_a, normed_a)), (row_b, edge_emit(hidden_b, normed_b))
    )):
        for m, (r, offset) in enumerate(((0, 1), (rows - 1, 2 - rows))):
            jobs += spatial_jobs(get_row, [(r, 1)], offset, shifted.at[2 * n + m], sums, 2 * n + m,
                                 kernel, weights, emit)
    run(jobs)
    product = jnp.dot(normed_a[...].reshape(-1, normed_a.shape[-1]), time_kernel[2],
                      preferred_element_type=F32)
    product_a[...] = product.astype(BF16).reshape(product_a.shape)


def main_kernel(counts, edges, inners, got_0, got_1, kernel, space_gain, space_bias, time_gain,
                time_kernel, time_bias, hidden_be, hidden_bi, normed_be, normed_bi, hidden_ae, normed_ae, *refs):
    *inner_a, out_ref, base, shifted, sums, normed_p, decoded, sems = refs
    hidden_ai, normed_ai = inner_a[::2], inner_a[1::2]
    rows, cols, channels = base.shape
    keep = jnp.where(lax.axis_index("frame") > 0, 1.0, 0.0)

    def emit(first, count, hidden, normed):
        normed_p[first : first + count] = (normed * keep).astype(BF16).reshape(count, cols, channels)

    def rows_of(first, count, *parts):
        get_row = framed(None, *parts, None)
        return jnp.concatenate([get_row(r) for r in range(first, first + count)], axis=0)

    def out_rows(first, count):
        prior = normed_p[first : first + count].reshape(count * cols, channels)
        total = rows_of(first, count, hidden_be, hidden_bi) + time_bias[...]
        total += (
            jnp.dot(rows_of(first, count, normed_be, normed_bi), time_kernel[0], preferred_element_type=F32)
            + jnp.dot(rows_of(first, count, normed_ae, normed_ai), time_kernel[1], preferred_element_type=F32)
            + jnp.dot(prior, time_kernel[2], preferred_element_type=F32)
        )
        decoded[first : first + count] = total.astype(BF16).reshape(count, cols, channels)

    def base_rows(first, count):
        prior = normed_p[first : first + count].reshape(count * cols, channels)
        total = rows_of(first, count, hidden_ae, hidden_ai) + time_bias[...]
        total += (
            jnp.dot(rows_of(first, count, normed_ae, normed_ai), time_kernel[0], preferred_element_type=F32)
            + jnp.dot(prior, time_kernel[1], preferred_element_type=F32)
        )
        return total

    halo = functools.partial(halo_row, counts, got_0, got_1, 2)
    get_row = framed(lambda: halo(True), edges, inners, lambda: halo(False))
    run(spatial_jobs(get_row, blocks(0, rows), 1, shifted, sums, 0, kernel,
                     (space_gain, space_bias, time_gain), emit))
    copies = []
    for n, (first, count) in enumerate(blocks(0, rows)):
        out_rows(first, count)
        copies.append(pltpu.make_async_copy(
            decoded.at[pl.ds(first, count)], out_ref.at[1, pl.ds(first, count)], sems.at[n]))
        copies[-1].start()
    for first, count in blocks(0, rows):
        base[first : first + count] = base_rows(first, count).reshape(count, cols, channels)
    for copy in copies:
        copy.wait()


def ends_late(count):
    index = lax.axis_index("frame")
    return jnp.logical_and(lax.rem(index, 2) == 0, index > 0) if count % 2 == 0 else index >= 0


def write_edges(products, base, out_ref, edges, sems):
    rows = base.shape[0]
    keep = jnp.where(lax.axis_index("frame") > 0, 1.0, 0.0)
    copies = []
    for n, row in enumerate((0, rows - 1)):
        edges[n] = (base[row] + products[n].astype(F32) * keep).astype(BF16)
        copies.append(pltpu.make_async_copy(edges.at[pl.ds(n, 1)], out_ref.at[0, pl.ds(row, 1)], sems.at[n]))
        copies[-1].start()
    for copy in copies:
        copy.wait()


def inner_finish_kernel(frames, base, time_kernel, products, *refs):
    *arrived, _, out_ref, decoded, edges, sems = refs
    cols, channels = base.shape[1:]
    keep = jnp.where(lax.axis_index("frame") > 0, 1.0, 0.0)
    kernel = (time_kernel[2].astype(F32) * keep).astype(BF16)
    start = 1
    copies = []
    for part in arrived:
        for row, count in blocks(start, start + part.shape[0]):
            normed = part[pl.ds(row - start, count)].reshape(count * cols, channels)
            total = base[row : row + count].reshape(count * cols, channels)
            total += jnp.dot(normed, kernel, preferred_element_type=F32)
            at = pl.ds(row - 1, count)
            decoded[at] = total.astype(BF16).reshape(count, cols, channels)
            copies.append(pltpu.make_async_copy(
                decoded.at[at], out_ref.at[0, pl.ds(row, count)], sems.at[2 + len(copies)]))
            copies[-1].start()
        start += part.shape[0]
    pl.when(jnp.logical_not(ends_late(frames)))(lambda: write_edges(products, base, out_ref, edges, sems))
    for copy in copies:
        copy.wait()


def finish_kernel(frames, products, base, _, out_ref, edges, sems):
    pl.when(ends_late(frames))(lambda: write_edges(products, base, out_ref, edges, sems))


def cost(pixels, taps, channels, arrays):
    return pl.CostEstimate(
        flops=2 * pixels * taps * channels * channels,
        bytes_accessed=2 * arrays * pixels * channels,
        transcendentals=2 * pixels * channels,
    )


def body(features, space_kernel, space_gain, space_bias, time_kernel, time_gain, time_bias):
    frames, rows, cols, channels = features.shape
    row = (cols, channels)
    count_f, count_b = lax.axis_size("frame"), lax.axis_size("band")
    counts = (count_f, count_b)
    onward = [(i, (i + 1) % count_f) for i in range(count_f)]
    ring = halo_ring(count_f, count_b)

    def shape(*lead, dtype=BF16):
        return jax.ShapeDtypeStruct(tuple(lead) + row, dtype)

    def room(*lead, dtype=BF16):
        return pltpu.VMEM(tuple(lead) + row, dtype)

    space_gain = space_gain.reshape(1, channels)
    time_gain = time_gain.reshape(1, channels)
    space_bias = space_bias.reshape(1, channels)
    time_bias = time_bias.reshape(1, channels)
    sums = pltpu.VMEM((4, STEP * cols, channels), F32)

    weights = (space_gain, space_bias, time_gain)
    count = len(blocks(0, rows))

    def call(kernel, inputs, outs, scratch, mebibytes, name, **more):
        inputs = [x if isinstance(x, tuple) else (VMEM, x) for x in inputs]
        specs, arrays = zip(*inputs)
        out_specs, out_shape = zip(*((VMEM, o) if not isinstance(o, tuple) else o for o in outs))
        arrays = [x if x.ndim < 3 or s is ANY else pltpu.with_memory_space_constraint(x, s.memory_space)
                  for s, x in zip(specs, arrays)]
        out_shape = [pltpu.VMEM(o.shape, o.dtype) if s is VMEM else o for s, o in zip(out_specs, out_shape)]
        return pl.pallas_call(
            kernel, in_specs=list(specs), out_specs=list(out_specs), out_shape=out_shape,
            scratch_shapes=scratch, name=name,
            compiler_params=pltpu.CompilerParams(vmem_limit_bytes=mebibytes * 1024 * 1024), **more,
        )(*arrays)

    def inner_rows(raw, start, n, scale, name, after):
        return call(
            functools.partial(inner_kernel, start), [(ANY, after), *raw, space_kernel, *weights],
            [shape(n, dtype=F32), shape(n)], [room(3, n + 2), sums],
            6, name, cost_estimate=cost(n * cols, 9 * scale, channels, 3),
        )

    held = 3 if rows >= 6 else 2
    (ends,) = call(
        functools.partial(ends_kernel, count_f), [(HBM, features)], [shape(held)],
        [pltpu.SemaphoreType.DMA((2,))], 1, "ends",
    )
    edge = [lax.ppermute(ends, "frame", onward)]
    edge_out, inner_out = call(
        load_kernel, [(ANY, ends), (HBM, features)], [shape(held), shape(rows - held)],
        [pltpu.SemaphoreType.DMA((3,))], 1, "load",
    )
    raw_a, space_kernel, time_kernel = call(
        load_rest_kernel, [(ANY, inner_out), (HBM, features), (HBM, space_kernel), (HBM, time_kernel)],
        [shape(rows), jax.ShapeDtypeStruct(space_kernel.shape, BF16),
         jax.ShapeDtypeStruct(time_kernel.shape, BF16)],
        [pltpu.SemaphoreType.DMA((3,))], 1, "load_rest",
    )
    inner = lax.ppermute(inner_out, "frame", onward)
    if count_f % 2 == 0:
        edge.append(lax.ppermute(edge_out, "frame", [(f, f ^ 1) for f in range(count_f)]))

    ring_rows = min(RING_ROWS, (rows - 2 - STEP) // STEP * STEP)
    parts = [rows - 2 - ring_rows] + [ring_rows] * (ring_rows > 0)
    inner_a = []
    if ring_rows:
        inner_a = inner_rows([raw_a], 1 + parts[0], ring_rows, 1, "inner_a_ring", raw_a)
    (edge[0],) = call(copy_kernel, [edge[0]], [shape(held)], [], 1, "arrived")
    edge, send_0, send_1 = call(
        functools.partial(halo_kernel, count_f), [raw_a, edge_out, *edge],
        [shape(held), shape(3), shape(3)], [], 1, "halo",
    )
    inner_a = [*inner_rows([raw_a], 1, parts[0], 8, "inner_a", send_0), *inner_a]
    normed_ai = inner_a[1::2]
    got_0 = lax.ppermute(send_0, ("frame", "band"), ring)
    got_1 = lax.ppermute(send_1, ("frame", "band"), [(t, s) for s, t in ring])
    arrived = [lax.ppermute(normed_ai[0], "frame", onward[:-1])]
    arrived += [lax.ppermute(part, "frame", onward) for part in normed_ai[1:]]
    hidden_bi, normed_bi = inner_rows([edge_out, inner_out], 1, rows - 2, 1, "inner_b", normed_ai[0])
    hidden_ae, normed_ae, hidden_be, normed_be, product_ae = call(
        functools.partial(edges_kernel, counts), [raw_a, edge_out, inner_out, got_0, got_1, space_kernel, *weights,
         time_kernel],
        [shape(2, dtype=F32), shape(2)] * 2 + [shape(2)], [room(4, 3, 3), sums],
        4, "edges", cost_estimate=cost(4 * cols, 9, channels, 3),
    )
    edge_arrived = lax.ppermute(product_ae, "frame", onward)
    edge_swapped = edge_arrived
    if count_f % 2 == 0:
        edge_swapped = lax.ppermute(product_ae, "frame", [(f, f ^ 1) for f in range(count_f)])

    decoded, base = call(
        functools.partial(main_kernel, counts),
        [edge, inner, got_0, got_1, space_kernel, *weights, time_kernel, time_bias,
         hidden_be, hidden_bi, normed_be, normed_bi, hidden_ae, normed_ae, *inner_a],
        [(ANY, jax.ShapeDtypeStruct(features.shape, BF16)), shape(rows, dtype=F32)],
        [room(3, rows + 2), sums, room(rows), room(rows), pltpu.SemaphoreType.DMA((count,))],
        9, "main", cost_estimate=cost(rows * cols, 14 * 8, channels, 10),
    )
    out = (ANY, jax.ShapeDtypeStruct(features.shape, BF16))
    (decoded,) = call(
        functools.partial(inner_finish_kernel, count_f),
        [base, time_kernel, edge_swapped, *arrived, (ANY, decoded)], [out],
        [room(rows - 2), room(2), pltpu.SemaphoreType.DMA((rows,))],
        3, "inner_finish", input_output_aliases={3 + len(arrived): 0},
        cost_estimate=cost(rows * cols, 1, channels, 4),
    )
    (decoded,) = call(
        functools.partial(finish_kernel, count_f), [edge_arrived, base, (ANY, decoded)], [out],
        [room(2), pltpu.SemaphoreType.DMA((2,))],
        3, "finish", input_output_aliases={2: 0}, cost_estimate=cost(2 * cols, 1, channels, 4),
    )
    return decoded


def solution(mesh):
    return jax.shard_map(
        body,
        mesh=mesh,
        in_specs=(P(("grp", "frame"), "band", None, None), P(), P(), P(), P(), P(), P()),
        out_specs=P(("grp", "frame"), "band", None, None),
        check_vma=False,
    )
```

```python
import functools

import jax
import jax.numpy as jnp
from jax import lax
from jax.experimental import pallas as pl
from jax.experimental.pallas import tpu as pltpu
from jax.sharding import PartitionSpec as P

F32 = jnp.float32
BF16 = jnp.bfloat16
VMEM = pl.BlockSpec(memory_space=pltpu.VMEM)
ANY = pl.BlockSpec(memory_space=pl.ANY)
HBM = pl.BlockSpec(memory_space=pltpu.HBM)
STEP = 2
RING_ROWS = 4


def blocks(first, last):
    return [(r, min(STEP, last - r)) for r in range(first, last, STEP)]


def rms_silu(values, gain):
    mean_square = jnp.mean(values * values, axis=-1, keepdims=True)
    u = values * lax.rsqrt(mean_square + 1e-06) * (0.5 * gain)
    return u + u * jnp.tanh(u)


def norm_into(shifted, place, row, gain):
    row, scale = row if isinstance(row, tuple) else (row, None)
    normed = rms_silu(row.astype(F32), gain)
    normed = normed if scale is None else normed * scale
    cols = normed.shape[0]
    column = lax.broadcasted_iota(jnp.int32, normed.shape, 0)
    before = jnp.where(column == 0, 0.0, pltpu.roll(normed, 1, 0))
    after = jnp.where(column == cols - 1, 0.0, pltpu.roll(normed, cols - 1, 0))
    shifted[0, place] = before.astype(BF16)
    shifted[1, place] = normed.astype(BF16)
    shifted[2, place] = after.astype(BF16)


def conv_rows(shifted, kernel, place, count):
    cols, channels = shifted.shape[2:]
    total = None
    for i in range(3):
        for j in range(3):
            window = shifted[j, place + i : place + i + count].reshape(count * cols, channels)
            product = jnp.dot(window, kernel[i, j], preferred_element_type=F32)
            total = product if total is None else total + product
    return total


def spatial_jobs(get_row, row_blocks, offset, shifted, sums, slot0, kernel, weights, emit, after=None):
    space_gain, space_bias, time_gain = weights
    ready = set()
    jobs = []

    def norm_stage(first, count):
        for r in range(first - 1, first + count + 1):
            if r not in ready:
                ready.add(r)
                norm_into(shifted, r + offset, get_row(r), space_gain[...])

    def conv_stage(slot, first, count):
        total = conv_rows(shifted, kernel, first - 1 + offset, count)
        sums[slot, : total.shape[0]] = total

    def emit_stage(slot, first, count):
        own = jnp.concatenate([get_row(r) for r in range(first, first + count)], axis=0)
        hidden = own.astype(F32) + sums[slot, : own.shape[0]] + space_bias[...]
        emit(first, count, hidden, rms_silu(hidden, time_gain[...]))

    for n, (first, count) in enumerate(row_blocks):
        slot = (slot0 + n) % sums.shape[0]
        jobs.append([
            functools.partial(norm_stage, first, count),
            functools.partial(conv_stage, slot, first, count),
            functools.partial(emit_stage, slot, first, count),
            functools.partial(after, first, count) if after else None,
        ])
    return jobs


def run(jobs):
    for n in range(len(jobs) + 3):
        for stage in range(4):
            if 0 <= n - stage < len(jobs) and jobs[n - stage][stage] is not None:
                jobs[n - stage][stage]()


def wait_all(pairs, sems):
    copies = [pltpu.make_async_copy(a, b, sems.at[n]) for n, (a, b) in enumerate(pairs)]
    for copy in copies:
        copy.start()
    for copy in copies:
        copy.wait()


def end_pairs(feats, ends):
    rows, lower = feats.shape[1], ends.shape[0] // 2
    upper = ends.shape[0] - lower
    return [
        (feats.at[1, pl.ds(0, upper)], ends.at[pl.ds(0, upper)]),
        (feats.at[1, pl.ds(rows - lower, lower)], ends.at[pl.ds(upper, lower)]),
    ]


def ends_kernel(count, feats, ends, sems):
    first = first_of_pair(count)

    @pl.when(first)
    def _():
        ends[...] = jnp.zeros_like(ends)

    @pl.when(jnp.logical_not(first))
    def _():
        wait_all(end_pairs(feats, ends), sems)


def load_kernel(_, feats, ends, middle, sems):
    upper = ends.shape[0] - ends.shape[0] // 2
    wait_all(end_pairs(feats, ends) + [(feats.at[1, pl.ds(upper, middle.shape[0])], middle)], sems)


def load_rest_kernel(_, feats, kernel, time_kernel, raw_a, kernel_out, time_out, sems):
    wait_all([(feats.at[0], raw_a), (kernel, kernel_out), (time_kernel, time_out)], sems)


def goes_up(index, count):
    return index % 2 == 0 or count % 2 == 1


def halo_ring(frames, bands):
    paired = frames % 2 == 0
    pairs = []
    for f in range(frames):
        for b in range(bands):
            to = (f, b + 1) if goes_up(f, frames) else (f, b - 1)
            if not 0 <= to[1] < bands:
                if not paired:
                    continue
                to = (f ^ 1, b)
            pairs.append((f * bands + b, to[0] * bands + to[1]))
    return pairs


def up_first(count):
    index = lax.axis_index("frame")
    return lax.rem(index, 2) == 0 if count % 2 == 0 else index >= 0


def first_of_pair(count):
    index = lax.axis_index("frame")
    return lax.rem(index, 2) == 0 if count % 2 == 0 else index < 0


def copy_kernel(source, target):
    target[...] = source[...]


def halo_kernel(count, raw_a, edges_b, *refs):
    *arrived, edges, send_0, send_1 = refs
    rows = raw_a.shape[0]
    if len(arrived) == 1:
        edges[...] = arrived[0][...]
    else:
        first = first_of_pair(count)

        @pl.when(first)
        def _():
            edges[...] = arrived[0][...]

        @pl.when(jnp.logical_not(first))
        def _():
            edges[...] = arrived[1][...]

    last = edges.shape[0] - 1

    def fill(up_rows, down_rows):
        for n, (upper, lower) in enumerate((
            (raw_a.at[0], raw_a.at[rows - 1]), (edges_b.at[0], edges_b.at[last]), (edges.at[0], edges.at[last])
        )):
            up_rows[n] = lower[...]
            down_rows[n] = upper[...]

    up = up_first(count)
    pl.when(up)(lambda: fill(send_0, send_1))
    pl.when(jnp.logical_not(up))(lambda: fill(send_1, send_0))


def halo_row(counts, got_0, got_1, n, is_above):
    frames, bands = counts
    band = lax.axis_index("band")
    take = up_first(frames) if is_above else jnp.logical_not(up_first(frames))
    row = jnp.where(take, got_0[n].astype(F32), got_1[n].astype(F32))
    there = band > 0 if is_above else band < bands - 1
    return row, jnp.where(there, 1.0, 0.0)


def framed(upper, ends, middle, lower):
    middle = middle if isinstance(middle, list) else [middle]
    lower_ends, count = ends.shape[0] // 2, sum(part.shape[0] for part in middle)
    upper_ends = ends.shape[0] - lower_ends
    rows = ends.shape[0] + count

    def get_row(r):
        if r < 0 or r >= rows:
            return upper() if r < 0 else lower()
        if r < upper_ends or r >= rows - lower_ends:
            return ends[r if r < upper_ends else r - count]
        part, at = part_of(middle, r - upper_ends)
        return part[at]

    return get_row


def part_of(parts, row):
    for part in parts:
        if row < part.shape[0]:
            return part, row
        row -= part.shape[0]


def inner_emit(start, hidden_ref, normed_ref):
    def emit(first, count, hidden, normed):
        at = pl.ds(first - start, count)
        shape = (count,) + hidden_ref.shape[1:]
        hidden_ref[at] = hidden.astype(hidden_ref.dtype).reshape(shape)
        normed_ref[at] = normed.astype(BF16).reshape(shape)
    return emit


def edge_emit(hidden_ref, normed_ref):
    def emit(first, count, hidden, normed):
        which = 0 if first == 0 else 1
        hidden_ref[which] = hidden
        normed_ref[which] = normed.astype(BF16)
    return emit


def inner_kernel(start, _, *refs):
    *raw, kernel, space_gain, space_bias, time_gain, hidden_ref, normed_ref, shifted, sums = refs
    get_row = framed(None, *raw, None) if len(raw) == 2 else lambda r: raw[0][r]
    run(spatial_jobs(get_row, blocks(start, start + hidden_ref.shape[0]), 1 - start, shifted, sums, 0, kernel,
                     (space_gain, space_bias, time_gain), inner_emit(start, hidden_ref, normed_ref)))


def edges_kernel(counts, raw_a, edges_b, inners_b, got_0, got_1, kernel, space_gain, space_bias, time_gain,
                 time_kernel, hidden_a, normed_a, hidden_b, normed_b, product_a, shifted, sums):
    rows = raw_a.shape[0]
    weights = (space_gain, space_bias, time_gain)

    halo = functools.partial(halo_row, counts, got_0, got_1)

    def row_a(r):
        return halo(0, r < 0) if r < 0 or r >= rows else raw_a[r]

    row_b = framed(lambda: halo(1, True), edges_b, inners_b, lambda: halo(1, False))
    jobs = []
    for n, (get_row, emit) in enumerate((
        (row_a, edge_emit(hidden_a, normed_a)), (row_b, edge_emit(hidden_b, normed_b))
    )):
        for m, (r, offset) in enumerate(((0, 1), (rows - 1, 2 - rows))):
            jobs += spatial_jobs(get_row, [(r, 1)], offset, shifted.at[2 * n + m], sums, 2 * n + m,
                                 kernel, weights, emit)
    run(jobs)
    product = jnp.dot(normed_a[...].reshape(-1, normed_a.shape[-1]), time_kernel[2],
                      preferred_element_type=F32)
    product_a[...] = product.astype(BF16).reshape(product_a.shape)


def main_kernel(counts, edges, inners, got_0, got_1, kernel, space_gain, space_bias, time_gain,
                time_kernel, time_bias, hidden_be, hidden_bi, normed_be, normed_bi, hidden_ae, normed_ae, *refs):
    *inner_a, out_ref, base, shifted, sums, normed_p, decoded, sems = refs
    hidden_ai, normed_ai = inner_a[::2], inner_a[1::2]
    rows, cols, channels = base.shape
    keep = jnp.where(lax.axis_index("frame") > 0, 1.0, 0.0)

    def emit(first, count, hidden, normed):
        normed_p[first : first + count] = (normed * keep).astype(BF16).reshape(count, cols, channels)

    def rows_of(first, count, *parts):
        get_row = framed(None, *parts, None)
        return jnp.concatenate([get_row(r) for r in range(first, first + count)], axis=0)

    def out_rows(first, count):
        prior = normed_p[first : first + count].reshape(count * cols, channels)
        total = rows_of(first, count, hidden_be, hidden_bi) + time_bias[...]
        total += (
            jnp.dot(rows_of(first, count, normed_be, normed_bi), time_kernel[0], preferred_element_type=F32)
            + jnp.dot(rows_of(first, count, normed_ae, normed_ai), time_kernel[1], preferred_element_type=F32)
            + jnp.dot(prior, time_kernel[2], preferred_element_type=F32)
        )
        decoded[first : first + count] = total.astype(BF16).reshape(count, cols, channels)

    def base_rows(first, count):
        prior = normed_p[first : first + count].reshape(count * cols, channels)
        total = rows_of(first, count, hidden_ae, hidden_ai) + time_bias[...]
        total += (
            jnp.dot(rows_of(first, count, normed_ae, normed_ai), time_kernel[0], preferred_element_type=F32)
            + jnp.dot(prior, time_kernel[1], preferred_element_type=F32)
        )
        return total

    halo = functools.partial(halo_row, counts, got_0, got_1, 2)
    get_row = framed(lambda: halo(True), edges, inners, lambda: halo(False))
    run(spatial_jobs(get_row, blocks(0, rows), 1, shifted, sums, 0, kernel,
                     (space_gain, space_bias, time_gain), emit))
    copies = []
    for n, (first, count) in enumerate(blocks(0, rows)):
        out_rows(first, count)
        copies.append(pltpu.make_async_copy(
            decoded.at[pl.ds(first, count)], out_ref.at[1, pl.ds(first, count)], sems.at[n]))
        copies[-1].start()
    for first, count in blocks(0, rows):
        base[first : first + count] = base_rows(first, count).reshape(count, cols, channels)
    for copy in copies:
        copy.wait()


def ends_late(count):
    index = lax.axis_index("frame")
    return jnp.logical_and(lax.rem(index, 2) == 0, index > 0) if count % 2 == 0 else index >= 0


def write_edges(products, base, out_ref, edges, sems):
    rows = base.shape[0]
    keep = jnp.where(lax.axis_index("frame") > 0, 1.0, 0.0)
    copies = []
    for n, row in enumerate((0, rows - 1)):
        edges[n] = (base[row] + products[n].astype(F32) * keep).astype(BF16)
        copies.append(pltpu.make_async_copy(edges.at[pl.ds(n, 1)], out_ref.at[0, pl.ds(row, 1)], sems.at[n]))
        copies[-1].start()
    for copy in copies:
        copy.wait()


def inner_finish_kernel(frames, base, time_kernel, products, *refs):
    *arrived, _, out_ref, decoded, edges, sems = refs
    cols, channels = base.shape[1:]
    keep = jnp.where(lax.axis_index("frame") > 0, 1.0, 0.0)
    kernel = (time_kernel[2].astype(F32) * keep).astype(BF16)
    start = 1
    copies = []
    for part in arrived:
        for row, count in blocks(start, start + part.shape[0]):
            normed = part[pl.ds(row - start, count)].reshape(count * cols, channels)
            total = base[row : row + count].reshape(count * cols, channels)
            total += jnp.dot(normed, kernel, preferred_element_type=F32)
            at = pl.ds(row - 1, count)
            decoded[at] = total.astype(BF16).reshape(count, cols, channels)
            copies.append(pltpu.make_async_copy(
                decoded.at[at], out_ref.at[0, pl.ds(row, count)], sems.at[2 + len(copies)]))
            copies[-1].start()
        start += part.shape[0]
    pl.when(jnp.logical_not(ends_late(frames)))(lambda: write_edges(products, base, out_ref, edges, sems))
    for copy in copies:
        copy.wait()


def finish_kernel(frames, products, base, _, out_ref, edges, sems):
    pl.when(ends_late(frames))(lambda: write_edges(products, base, out_ref, edges, sems))


def cost(pixels, taps, channels, arrays):
    return pl.CostEstimate(
        flops=2 * pixels * taps * channels * channels,
        bytes_accessed=2 * arrays * pixels * channels,
        transcendentals=2 * pixels * channels,
    )


def body(features, space_kernel, space_gain, space_bias, time_kernel, time_gain, time_bias):
    frames, rows, cols, channels = features.shape
    row = (cols, channels)
    count_f, count_b = lax.axis_size("frame"), lax.axis_size("band")
    counts = (count_f, count_b)
    onward = [(i, (i + 1) % count_f) for i in range(count_f)]
    ring = halo_ring(count_f, count_b)

    def shape(*lead, dtype=BF16):
        return jax.ShapeDtypeStruct(tuple(lead) + row, dtype)

    def room(*lead, dtype=BF16):
        return pltpu.VMEM(tuple(lead) + row, dtype)

    space_gain = space_gain.reshape(1, channels)
    time_gain = time_gain.reshape(1, channels)
    space_bias = space_bias.reshape(1, channels)
    time_bias = time_bias.reshape(1, channels)
    sums = pltpu.VMEM((4, STEP * cols, channels), F32)

    weights = (space_gain, space_bias, time_gain)
    count = len(blocks(0, rows))

    def call(kernel, inputs, outs, scratch, mebibytes, name, **more):
        inputs = [x if isinstance(x, tuple) else (VMEM, x) for x in inputs]
        specs, arrays = zip(*inputs)
        out_specs, out_shape = zip(*((VMEM, o) if not isinstance(o, tuple) else o for o in outs))
        arrays = [x if x.ndim < 3 or s is ANY else pltpu.with_memory_space_constraint(x, s.memory_space)
                  for s, x in zip(specs, arrays)]
        out_shape = [pltpu.VMEM(o.shape, o.dtype) if s is VMEM else o for s, o in zip(out_specs, out_shape)]
        return pl.pallas_call(
            kernel, in_specs=list(specs), out_specs=list(out_specs), out_shape=out_shape,
            scratch_shapes=scratch, name=name,
            compiler_params=pltpu.CompilerParams(vmem_limit_bytes=mebibytes * 1024 * 1024), **more,
        )(*arrays)

    def inner_rows(raw, start, n, scale, name, after):
        return call(
            functools.partial(inner_kernel, start), [(ANY, after), *raw, space_kernel, *weights],
            [shape(n, dtype=F32), shape(n)], [room(3, n + 2), sums],
            6, name, cost_estimate=cost(n * cols, 9 * scale, channels, 3),
        )

    held = 3 if rows >= 6 else 2
    (ends,) = call(
        functools.partial(ends_kernel, count_f), [(HBM, features)], [shape(held)],
        [pltpu.SemaphoreType.DMA((2,))], 1, "ends",
    )
    edge = [lax.ppermute(ends, "frame", onward)]
    edge_out, inner_out = call(
        load_kernel, [(ANY, ends), (HBM, features)], [shape(held), shape(rows - held)],
        [pltpu.SemaphoreType.DMA((3,))], 1, "load",
    )
    raw_a, space_kernel, time_kernel = call(
        load_rest_kernel, [(ANY, inner_out), (HBM, features), (HBM, space_kernel), (HBM, time_kernel)],
        [shape(rows), jax.ShapeDtypeStruct(space_kernel.shape, BF16),
         jax.ShapeDtypeStruct(time_kernel.shape, BF16)],
        [pltpu.SemaphoreType.DMA((3,))], 1, "load_rest",
    )
    inner = lax.ppermute(inner_out, "frame", onward)
    if count_f % 2 == 0:
        edge.append(lax.ppermute(edge_out, "frame", [(f, f ^ 1) for f in range(count_f)]))

    ring_rows = min(RING_ROWS, (rows - 2 - STEP) // STEP * STEP)
    parts = [rows - 2 - ring_rows] + [ring_rows] * (ring_rows > 0)
    inner_a = []
    if ring_rows:
        inner_a = inner_rows([raw_a], 1 + parts[0], ring_rows, 1, "inner_a_ring", raw_a)
    (edge[0],) = call(copy_kernel, [edge[0]], [shape(held)], [], 1, "arrived")
    edge, send_0, send_1 = call(
        functools.partial(halo_kernel, count_f), [raw_a, edge_out, *edge],
        [shape(held), shape(3), shape(3)], [], 1, "halo",
    )
    inner_a = [*inner_rows([raw_a], 1, parts[0], 8, "inner_a", send_0), *inner_a]
    normed_ai = inner_a[1::2]
    got_0 = lax.ppermute(send_0, ("frame", "band"), ring)
    got_1 = lax.ppermute(send_1, ("frame", "band"), [(t, s) for s, t in ring])
    arrived = [lax.ppermute(normed_ai[0], "frame", onward[:-1])]
    arrived += [lax.ppermute(part, "frame", onward) for part in normed_ai[1:]]
    hidden_bi, normed_bi = inner_rows([edge_out, inner_out], 1, rows - 2, 1, "inner_b", normed_ai[0])
    hidden_ae, normed_ae, hidden_be, normed_be, product_ae = call(
        functools.partial(edges_kernel, counts), [raw_a, edge_out, inner_out, got_0, got_1, space_kernel, *weights,
         time_kernel],
        [shape(2, dtype=F32), shape(2)] * 2 + [shape(2)], [room(4, 3, 3), sums],
        4, "edges", cost_estimate=cost(4 * cols, 9, channels, 3),
    )
    edge_arrived = lax.ppermute(product_ae, "frame", onward)
    edge_swapped = edge_arrived
    if count_f % 2 == 0:
        edge_swapped = lax.ppermute(product_ae, "frame", [(f, f ^ 1) for f in range(count_f)])

    decoded, base = call(
        functools.partial(main_kernel, counts),
        [edge, inner, got_0, got_1, space_kernel, *weights, time_kernel, time_bias,
         hidden_be, hidden_bi, normed_be, normed_bi, hidden_ae, normed_ae, *inner_a],
        [(ANY, jax.ShapeDtypeStruct(features.shape, BF16)), shape(rows, dtype=F32)],
        [room(3, rows + 2), sums, room(rows), room(rows), pltpu.SemaphoreType.DMA((count,))],
        9, "main", cost_estimate=cost(rows * cols, 14 * 8, channels, 10),
    )
    out = (ANY, jax.ShapeDtypeStruct(features.shape, BF16))
    (decoded,) = call(
        functools.partial(inner_finish_kernel, count_f),
        [base, time_kernel, edge_swapped, *arrived, (ANY, decoded)], [out],
        [room(rows - 2), room(2), pltpu.SemaphoreType.DMA((rows,))],
        3, "inner_finish", input_output_aliases={3 + len(arrived): 0},
        cost_estimate=cost(rows * cols, 1, channels, 4),
    )
    (decoded,) = call(
        functools.partial(finish_kernel, count_f), [edge_arrived, base, (ANY, decoded)], [out],
        [room(2), pltpu.SemaphoreType.DMA((2,))],
        3, "finish", input_output_aliases={2: 0}, cost_estimate=cost(2 * cols, 1, channels, 4),
    )
    return decoded


def solution(mesh):
    return jax.shard_map(
        body,
        mesh=mesh,
        in_specs=(P(("grp", "frame"), "band", None, None), P(), P(), P(), P(), P(), P()),
        out_specs=P(("grp", "frame"), "band", None, None),
        check_vma=False,
    )
```
